512 devices in a mesh: lon: 64 (over x, z_hi, y, core), lat: 8 (over z_lo).
Axes of the slice: x: 4, y: 4, z: 16 (z_hi: 2, z_lo: 8; z = z_hi * 8 + z_lo), core: 2. Of those that a mesh axis runs over, the one named last changes fastest.
Arguments:
- latent_field: bfloat16 [2, 48, 768, 384], P(None, 'lat', 'lon'), may hold values from -6 to 6
- cotangent: bfloat16 [2, 48, 768, 384], P(None, 'lat', 'lon'), may hold values from -16 to 16
- norm_gain: float32 [384], replicated, may hold values from 0.1 to 1.9
- input_weight: bfloat16 [384, 1152], replicated, may hold values from -0.3125 to 0.3125
- output_weight: bfloat16 [384, 384], replicated, may hold values from -0.3125 to 0.3125
- bias_table: bfloat16 [8, 12, 3312], P('lat'), may hold values from -6 to 256
- regions: int32 [2, 48, 768], P(None, 'lat', 'lon'), may hold values from 0 to 3
Outputs:
- grad_field: bfloat16 [2, 48, 768, 384], P(None, 'lat', 'lon')
- grad_input_weight: bfloat16 [384, 1152], P('lon')
- grad_output_weight: bfloat16 [384, 384], P('lon')
- grad_gain: float32 [384], replicated
- grad_table: float32 [8, 12, 3312], P('lat')
The draws below stay inside these ranges and needn't reach their ends.
Inputs may be any that keep to these rules, and one draw needn't show every extreme that they name: `regions`: two cells of a window attend to each other only where their region ids agree.
All inputs are finite; a program needn't handle non-finite values.
Results may differ from the reference program's by a relative error of at most 0.02.
Values may be sent and summed in bfloat16 or wider, within the bound.
A program may use at most 128 MiB of HBM per device.

```python
import math
import jax
import jax.numpy as jnp
from jax import lax

D = 384
HEADS = 12
LEV = 2
WIN_LAT = 6
WIN_LON = 12
NLAT = 48
NLON = 768
TOKENS = 73728
TYPES = 8
POS = 3312


def draw_bias_table(key, part):
    key = jax.random.fold_in(key, 17)
    base_key = jax.random.fold_in(key, 0)
    shape_full = (TYPES, HEADS, POS)
    values = jnp.clip(jax.random.normal(base_key, shape_full, jnp.float32), -6.0, 6.0)
    return values.astype(jnp.bfloat16)


def plant(drawn, own_key, low, high):
    longest = drawn.shape.index(max(drawn.shape))
    spots = []
    for shift in (0, 1):
        where = [jax.random.randint(jax.random.fold_in(own_key, axis), (), 0, length) for axis, length in enumerate(drawn.shape)]
        where[longest] = (where[longest] + shift) % drawn.shape[longest]
        spots.append(tuple(where))
    return drawn.at[spots[0]].set(low).at[spots[1]].set(high)


def raised(array, stream_key, source, target, blocks, factor):
    owner, partner = [(jnp.arange(array.shape[axis_at]) // (array.shape[axis_at] // blocks)).reshape([-1 if axis == axis_at else 1 for axis in range(array.ndim)]) for axis_at in (source, target)]
    chosen = jax.random.permutation(stream_key, blocks)[partner]
    strong = (owner == chosen) | (owner == (partner + blocks // 2) % blocks)
    return jnp.where(strong, factor * array, array)


def level_of(own_key, shape, shards, smallest, top_value):
    level = 1.0
    for position, shards_of in shards:
        heights = jax.random.uniform(jax.random.fold_in(jax.random.fold_in(own_key, 6), position), (shards_of,), jnp.float32, smallest / len(shards), top_value / len(shards))
        level = level * jnp.repeat(jnp.exp(heights), shape[position] // shards_of).reshape((-1,) + (1,) * (len(shape) - 1 - position))
    return level


def bell_draw(own_key, extent, scale, limit, shards=(), held_as=jnp.bfloat16):
    loudness = level_of(own_key, extent, shards, -0.22, 0.18) if shards else 1.0
    drawn = jax.random.normal(own_key, extent, jnp.float32) * scale * loudness
    return jnp.minimum(jnp.maximum(drawn, -limit), limit).astype(held_as)


def heavy_noise(key, extent, scale, reach, pieces, heavy, dtype=jnp.bfloat16):
    array = scale * jax.random.normal(key, extent, jnp.float32)
    if pieces:
        array = array * level_of(key, extent, pieces, -0.22, 0.18)
    return jnp.clip(raised(array, jax.random.fold_in(key, 3), *heavy), -reach, reach).astype(dtype)


def setup_inputs(seed: int = 0) -> dict:
    keys = jax.random.split(jax.random.key(seed), 8)
    latent_field = bell_draw(keys[0], (LEV, NLAT, NLON, D), 1.0, 6.0, ((1, 8), (2, 64)))
    cotangent = heavy_noise(keys[1], (LEV, NLAT, NLON, D), 1.0, 16.0, ((1, 8), (2, 64)), (2, 3, 64, 4.0))
    norm_gain = jnp.clip(1.0 + 0.18 * jax.random.normal(keys[2], (D,), jnp.float32), 0.1, 1.9)
    input_weight = bell_draw(keys[3], (D, 3 * D), D ** -0.5, 0.3125)
    output_weight = bell_draw(keys[4], (D, D), D ** -0.5, 0.3125)
    bias_table = draw_bias_table(jax.random.fold_in(keys[7], 71), 0)
    regions = plant(jax.random.randint(keys[6], (LEV, NLAT, NLON), 0, 4), jax.random.fold_in(keys[6], 1), 0, 3).astype(jnp.int32)
    return dict(latent_field=latent_field, cotangent=cotangent, norm_gain=norm_gain, input_weight=input_weight, output_weight=output_weight, bias_table=bias_table, regions=regions)


norm_eps = 1e-05
masked_score = -1000000000.0
highest = lax.Precision.HIGHEST

def product(spec, left_arr, right_arr):
    return jnp.einsum(spec, left_arr.astype(jnp.float32), right_arr.astype(jnp.float32), precision=highest)

def longitude_onehot(span_cells):
    first_index = jnp.arange(span_cells)[:, None, None]
    second_index = jnp.arange(span_cells)[None, :, None]
    offset_index = jnp.arange(2 * span_cells - 1)[None, None, :]
    return (first_index - second_index + span_cells - 1 == offset_index).astype(jnp.float32)

def expand_bias(bias_rows):
    num_bands, num_heads = (bias_rows.shape[0], bias_rows.shape[1])
    shaped = bias_rows.astype(jnp.float32).reshape(num_bands, num_heads, LEV, LEV, WIN_LAT, WIN_LAT, 2 * WIN_LON - 1)
    spread = jnp.einsum('bhxyuvr,cdr->bhxucyvd', shaped, longitude_onehot(WIN_LON), precision=highest)
    window_cells = LEV * WIN_LAT * WIN_LON
    return spread.reshape(num_bands, num_heads, window_cells, window_cells)

def fold_bias(grad_full):
    num_bands, num_heads = (grad_full.shape[0], grad_full.shape[1])
    shaped = grad_full.reshape(num_bands, num_heads, LEV, WIN_LAT, WIN_LON, LEV, WIN_LAT, WIN_LON)
    folded = jnp.einsum('bhxucyvd,cdr->bhxyuvr', shaped, longitude_onehot(WIN_LON), precision=highest)
    return folded.reshape(num_bands, num_heads, -1)

def to_windows(cells_grid):
    levels, row_count, col_count = (cells_grid.shape[0], cells_grid.shape[1], cells_grid.shape[2])
    trailing = cells_grid.shape[3:]
    shaped = cells_grid.reshape((levels, row_count // WIN_LAT, WIN_LAT, col_count // WIN_LON, WIN_LON) + trailing)
    axes_order = (1, 3, 0, 2, 4) + tuple(range(5, 5 + len(trailing)))
    return jnp.transpose(shaped, axes_order).reshape((row_count // WIN_LAT, col_count // WIN_LON, levels * WIN_LAT * WIN_LON) + trailing)

def from_windows(blocks):
    num_bands, num_windows, features = (blocks.shape[0], blocks.shape[1], blocks.shape[3])
    shaped = blocks.reshape(num_bands, num_windows, LEV, WIN_LAT, WIN_LON, features)
    return jnp.transpose(shaped, (2, 0, 3, 1, 4, 5)).reshape(LEV, num_bands * WIN_LAT, num_windows * WIN_LON, features)

def window_grads(normed_win, grad_win, region_win, bias_rows, input_weight, output_weight):
    num_bands, num_windows, window_cells, features = normed_win.shape
    head_dim = features // HEADS
    score_scale = head_dim ** (-0.5)
    flat_normed = normed_win.reshape(-1, features)
    projected = jnp.dot(flat_normed, input_weight, preferred_element_type=jnp.float32).astype(jnp.bfloat16)
    projected = projected.reshape(num_bands, num_windows, window_cells, 3, HEADS, head_dim)
    queries, key_rows, values = (projected[:, :, :, 0], projected[:, :, :, 1], projected[:, :, :, 2])
    scores = product('bwihe,bwjhe->bwhij', queries, key_rows) * score_scale
    scores = scores + expand_bias(bias_rows)[:, None]
    same_region = region_win[:, :, :, None] == region_win[:, :, None, :]
    scores = jnp.where(same_region[:, :, None], scores, masked_score)
    softmax_out = jax.nn.softmax(scores, axis=-1)
    probs_low = softmax_out.astype(jnp.bfloat16)
    attended = product('bwhij,bwjhe->bwihe', probs_low, values).astype(jnp.bfloat16)
    flat_attended = attended.reshape(-1, features)
    flat_grad = grad_win.reshape(-1, features)
    grad_attended = jnp.dot(flat_grad, output_weight.T, preferred_element_type=jnp.float32).astype(jnp.bfloat16)
    grad_attended = grad_attended.reshape(num_bands, num_windows, window_cells, HEADS, head_dim)
    grad_probs = product('bwihe,bwjhe->bwhij', grad_attended, values)
    grad_values = product('bwhij,bwihe->bwjhe', probs_low, grad_attended)
    grad_scores = softmax_out * (grad_probs - lax.optimization_barrier(jnp.sum(softmax_out * grad_probs, axis=-1, keepdims=True)))
    grad_table = fold_bias(lax.optimization_barrier(jnp.sum(grad_scores, axis=1)))
    scores_low = (grad_scores * score_scale).astype(jnp.bfloat16)
    grad_queries = product('bwhij,bwjhe->bwihe', scores_low, key_rows)
    grad_keys = product('bwhij,bwihe->bwjhe', scores_low, queries)
    grad_projected = jnp.stack([grad_queries, grad_keys, grad_values], axis=3).astype(jnp.bfloat16)
    grad_projected = grad_projected.reshape(-1, 3 * features)
    grad_normed = jnp.dot(grad_projected, input_weight.T, preferred_element_type=jnp.float32).astype(jnp.bfloat16)
    return (grad_normed.reshape(normed_win.shape), flat_normed, grad_projected, flat_attended, flat_grad, grad_table)

def reference(latent_field, cotangent, norm_gain, input_weight, output_weight, bias_table, regions):
    field_f32 = latent_field.astype(jnp.float32)
    centred = field_f32 - lax.optimization_barrier(jnp.mean(field_f32, axis=-1, keepdims=True))
    inv_std = lax.rsqrt(lax.optimization_barrier(jnp.mean(centred * centred, axis=-1, keepdims=True)) + norm_eps)
    normalized = centred * inv_std
    normed = (normalized * norm_gain).astype(jnp.bfloat16)
    shifts = (-(LEV // 2), -(WIN_LAT // 2), -(WIN_LON // 2))
    normed_shift = jnp.roll(normed, shifts, axis=(0, 1, 2))
    grad_shift = jnp.roll(cotangent, shifts, axis=(0, 1, 2))
    normed_win = to_windows(normed_shift)
    grad_win = to_windows(grad_shift)
    region_win = to_windows(regions)
    features = latent_field.shape[3]

    def one_band(running, band_item):
        normed_band, grad_band, region_band, table_band = band_item
        results = window_grads(normed_band[None], grad_band[None], region_band[None], table_band[None], input_weight, output_weight)
        grad_normed, flat_normed, grad_projected, flat_attended, flat_grad, grad_table = results
        weight_in = running[0] + jnp.dot(flat_normed.T, grad_projected, preferred_element_type=jnp.float32)
        weight_out = running[1] + jnp.dot(flat_attended.T, flat_grad, preferred_element_type=jnp.float32)
        return ((weight_in, weight_out), (grad_normed[0], grad_table[0]))
    initial = (jnp.zeros((features, 3 * features), jnp.float32), jnp.zeros((features, features), jnp.float32))
    sums, outputs = lax.scan(one_band, initial, (normed_win, grad_win, region_win, bias_table))
    grad_windows, grad_table = outputs
    grad_shifted = from_windows(grad_windows)
    grad_normed = jnp.roll(grad_shifted, (LEV // 2, WIN_LAT // 2, WIN_LON // 2), axis=(0, 1, 2))
    grad_f32 = grad_normed.astype(jnp.float32)
    scaled = grad_f32 * norm_gain
    grad_field = cotangent.astype(jnp.float32) + inv_std * (scaled - lax.optimization_barrier(jnp.mean(scaled, axis=-1, keepdims=True)) - normalized * lax.optimization_barrier(jnp.mean(scaled * normalized, axis=-1, keepdims=True)))
    factor = 1.0 / math.sqrt(TOKENS)
    grad_gain = lax.optimization_barrier(jnp.sum(grad_f32 * normalized, axis=(0, 1, 2))) * factor
    return (grad_field.astype(jnp.bfloat16), (sums[0] * factor).astype(jnp.bfloat16), (sums[1] * factor).astype(jnp.bfloat16), grad_gain, grad_table)
```

```python
import functools
import math

import jax
import jax.numpy as jnp
import numpy as np
from jax import lax
from jax.experimental import pallas as pl
from jax.experimental.pallas import tpu as pltpu
from jax.sharding import PartitionSpec as P

D = 384
HEADS = 12
HEAD_DIM = 32
LEV = 2
WIN_LAT = 6
WIN_LON = 12
CELLS = 144
ROWS = LEV * WIN_LAT
QUAD = 36
SLOT = 80
BACK = 48
SPREAD = 2 * WIN_LON - 1
HALF_POS = WIN_LAT * SPREAD
POS = 3312
WIDE = 256
CHUNK = 10
CHIPS = 16
CORE_TILES = 16
GAIN_TILE = 26
SCATTER = WIN_LON * ROWS * 16

norm_eps = 1e-05
masked_score = -1000000000.0
VMEM = pltpu.VMEM
f32 = jnp.float32
bf16 = jnp.bfloat16


def quad_of(p):
    lon, lev, lat = p // ROWS, (p % ROWS) // WIN_LAT, p % WIN_LAT
    quad = (lat // 3) * 2 + lon // 6
    return quad, (lev * 3 + lat % 3) * 6 + lon % 6


def gather_matrices():
    field = np.zeros((CELLS, 4 * SLOT), np.float32)
    cot = np.zeros((CELLS, 4 * SLOT), np.float32)
    back = np.zeros((4 * BACK, CELLS), np.float32)
    for p in range(CELLS):
        quad, place = quad_of(p)
        field[p, quad * SLOT + place] = 1
        cot[p, quad * SLOT + QUAD + place] = 1
        back[quad * BACK + place, p] = 1
    return field, cot, back


def feature_order():
    out = np.zeros((D, D), np.float32)
    r = 0
    for core in range(2):
        for x in range(4):
            for z_hi in range(2):
                for y in range(4):
                    lon = ((x * 2 + z_hi) * 4 + y) * 2 + core
                    for k in range(6):
                        out[r, lon * 6 + k] = 1
                        r += 1
    return out


def bias_selectors():
    out = np.zeros((WIN_LON, 2 * HALF_POS, WIDE), np.float32)
    for c in range(WIN_LON):
        for p in range(CELLS):
            d, yv = p // ROWS, p % ROWS
            out[c, (yv // WIN_LAT) * HALF_POS + (yv % WIN_LAT) * SPREAD + c - d + WIN_LON - 1, p] = 1
    return out


def head_rows(ref, h):
    return jnp.concatenate(
        [ref[pl.ds(half * SCATTER + h, CELLS, stride=16), :] for half in range(2)], axis=1
    )


def put_head_rows(ref, h, value):
    for half in range(2):
        ref[pl.ds(half * SCATTER + h, CELLS, stride=16), :] = value[:, half * 128 : half * 128 + 128]


def nt(a, b):
    return lax.dot_general(a, b, (((1,), (1,)), ((), ())), preferred_element_type=f32)


def nn(a, b):
    return lax.dot_general(a, b, (((1,), (0,)), ((), ())), preferred_element_type=f32)


def tn(a, b):
    return lax.dot_general(a, b, (((0,), (0,)), ((), ())), preferred_element_type=f32)


def iota(shape, dim):
    return lax.broadcasted_iota(jnp.int32, shape, dim)


def expand_table(table_ref, sel_ref, tprime, bias):
    table = table_ref[0].astype(f32)
    tprime[...] = jnp.zeros_like(tprime)
    for xu in range(ROWS):
        x, u = xu // WIN_LAT, xu % WIN_LAT
        for y in range(2):
            off = ((x * 2 + y) * WIN_LAT + u) * HALF_POS
            tprime[xu * 16 : xu * 16 + HEADS, y * HALF_POS : (y + 1) * HALF_POS] = table[
                :, off : off + HALF_POS
            ]
    rows = tprime[...].astype(bf16)
    for c in range(WIN_LON):
        part = nn(rows, sel_ref[c])
        for half in range(2):
            base = half * SCATTER + c * 192
            bias[base : base + 192, :] = part[:, half * 128 : half * 128 + 128]


def same_region(reg_ref, regs):
    regs[0:WIN_LAT, 0:WIN_LON] = reg_ref[0].astype(f32)
    regs[WIN_LAT:ROWS, 0:WIN_LON] = reg_ref[1].astype(f32)
    grid = regs[0:ROWS, 0:WIN_LON].astype(bf16)
    place = iota((ROWS, WIDE), 1)
    spread = nn(grid, (place // ROWS == iota((ROWS, WIDE), 0)).astype(bf16))
    row = jnp.sum(
        jnp.where(place % ROWS == iota((ROWS, WIDE), 0), spread, 0.0), axis=0, keepdims=True
    )
    kind = iota((16, WIDE), 0).astype(f32)
    hot = jnp.where((row == kind) & (iota((16, WIDE), 1) < CELLS), 1.0, 0.0)
    return tn(hot[:, :CELLS].astype(bf16), hot.astype(bf16)) > 0.5


def pad_cells(a):
    return jnp.concatenate([a, jnp.zeros((WIDE - CELLS, a.shape[1]), a.dtype)], axis=0)


def window_math(
    win, gain_ref, win_ref, wout_ref, reg_ref, sel_ref, field_ref, cot_ref, back_ref, feat_ref,
    out_back, out_sums, out_tiles_store, bias, dsf, dpt, att, tabf, regs, qkv_s,
):
    scale = HEAD_DIM ** -0.5
    cells = nn(field_ref[...], win)
    cot = nn(cot_ref[...], win)
    cot_low = cot.astype(bf16)
    centred = cells - jnp.mean(cells, axis=1, keepdims=True)
    inv_std = lax.rsqrt(jnp.mean(centred * centred, axis=1, keepdims=True) + norm_eps)
    normalized = centred * inv_std
    gain = gain_ref[...]
    normed = (normalized * gain).astype(bf16)
    qkv_s[:, : 3 * D] = nn(normed, win_ref[...]).astype(bf16)
    qkv_s[:, 3 * D :] = nt(cot_low, wout_ref[...]).astype(bf16)
    normed_t = nt(feat_ref[...], normed).astype(bf16)
    eye = (iota((128, 128), 0) == iota((128, 128), 1)).astype(bf16)
    same = same_region(reg_ref, regs)
    lane = iota((CELLS, 128), 1) // HEAD_DIM

    for g in range(3):
        lo = g * 128
        q = qkv_s[:, lo : lo + 128]
        k = pad_cells(qkv_s[:, D + lo : D + lo + 128])
        v = pad_cells(qkv_s[:, 2 * D + lo : 2 * D + lo + 128])
        do = qkv_s[:, 3 * D + lo : 3 * D + lo + 128]
        q_t = nt(eye, q).astype(bf16)
        k_t = nt(eye, k).astype(bf16)
        v_t = nt(eye, v).astype(bf16)
        do_t = nt(eye, do).astype(bf16)
        zero = jnp.zeros_like(q)
        for e in range(4):
            h = g * 4 + e
            r = e * HEAD_DIM
            mine = lane == e
            s = nt(jnp.where(mine, q, zero), k) * scale + head_rows(bias, h)
            s = jnp.where(same, s, masked_score)
            s = jnp.exp(s - jnp.max(s, axis=1, keepdims=True))
            p = s * (1.0 / jnp.sum(s, axis=1, keepdims=True))
            p_low = p.astype(bf16)
            att[h * 32 : h * 32 + 32, :] = nt(v_t[r : r + 32], p_low).astype(bf16)
            dp = nt(jnp.where(mine, do, zero), v)
            dpt[2 * D + h * 32 : 2 * D + h * 32 + 32, :] = nn(do_t[r : r + 32], p_low)[
                :, :CELLS
            ].astype(bf16)
            ds = p * (dp - jnp.sum(p * dp, axis=1, keepdims=True))
            put_head_rows(dsf, h, ds)
            ds_low = (ds * scale).astype(bf16)
            dpt[h * 32 : h * 32 + 32, :] = nt(k_t[r : r + 32], ds_low).astype(bf16)
            dpt[D + h * 32 : D + h * 32 + 32, :] = nn(q_t[r : r + 32], ds_low)[:, :CELLS].astype(
                bf16
            )
    for h in range(HEADS, 16):
        put_head_rows(dsf, h, jnp.zeros((CELLS, WIDE), f32))

    att_t = nn(feat_ref[...], att[...]).astype(bf16)
    for b in range(4):
        if b < 3:
            block = nt(normed_t, dpt[b * D : (b + 1) * D, :]).astype(bf16)
        else:
            block = nn(att_t, cot_low).astype(bf16)
        for core in range(2):
            for x in range(4):
                r = (core * 4 + x) * 48
                for t in range(3):
                    out_sums[core, x * 4 + b, t * 3 : t * 3 + 3] = block[
                        r : r + 48, t * 128 : t * 128 + 128
                    ].reshape(3, 16, 128)

    shifted_t = nn(win_ref[...], dpt[...]).astype(bf16)
    eye_c = (iota((CELLS, CELLS), 0) == iota((CELLS, CELLS), 1)).astype(bf16)
    g_normed = nt(eye_c, shifted_t)
    scaled = g_normed * gain
    grad = cot + inv_std * (
        scaled
        - jnp.mean(scaled, axis=1, keepdims=True)
        - normalized * jnp.mean(scaled * normalized, axis=1, keepdims=True)
    )
    out_back[...] = nn(back_ref[...], grad.astype(bf16)).astype(bf16).reshape(4, BACK, D)
    grad_gain = jnp.sum(g_normed * normalized, axis=0, keepdims=True)

    acc = jnp.zeros((192, 2 * HALF_POS), f32)
    for c in range(WIN_LON):
        part = jnp.concatenate(
            [dsf[pl.ds(half * SCATTER + c * 192, 192), :] for half in range(2)], axis=1
        )
        acc = acc + nt(part.astype(bf16), sel_ref[c])
    tabf[:, 25 * 128 : 32 * 128] = jnp.zeros((16, 7 * 128), f32)
    for xu in range(ROWS):
        x, u = xu // WIN_LAT, xu % WIN_LAT
        for y in range(2):
            off = ((x * 2 + y) * WIN_LAT + u) * HALF_POS
            tabf[:, off : off + HALF_POS] = acc[
                xu * 16 : xu * 16 + 16, y * HALF_POS : (y + 1) * HALF_POS
            ]
    for k in range(3):
        tabf[k : k + 1, GAIN_TILE * 128 : GAIN_TILE * 128 + 128] = grad_gain[
            :, k * 128 : k * 128 + 128
        ]
    for t in range(32):
        out_sums[t // 16, t % 16, 9] = tabf[:, t * 128 : t * 128 + 128].astype(bf16)


def local_kernel(
    win_r, gain_ref, win_ref, wout_ref, table_ref, reg_ref, sel_ref, field_ref, cot_ref, back_ref,
    feat_ref, out_back, out_sums, tprime, bias, dsf, dpt, att, tabf, regs, qkv_s,
):
    expand_table(table_ref, sel_ref, tprime, bias)
    window_math(
        win_r[...].reshape(4 * SLOT, D), gain_ref, win_ref, wout_ref, reg_ref, sel_ref, field_ref,
        cot_ref, back_ref, feat_ref, out_back, out_sums, None, bias, dsf, dpt, att, tabf, regs,
        qkv_s,
    )


LOCAL_SCRATCH = [
    VMEM((192, 2 * HALF_POS), f32),
    VMEM((2 * SCATTER, 128), f32),
    VMEM((2 * SCATTER, 128), f32),
    VMEM((3 * D, CELLS), bf16),
    VMEM((D, CELLS), bf16),
    VMEM((16, 32 * 128), f32),
    VMEM((16, 128), f32),
    VMEM((CELLS, 4 * D), bf16),
]


def local_call(win, norm_gain, input_weight, output_weight, bias_table, regions):
    field, cot, back = gather_matrices()
    consts = [jnp.asarray(a, bf16) for a in (bias_selectors(), field, cot, back, feature_order())]
    return pl.pallas_call(
        local_kernel,
        out_shape=(
            jax.ShapeDtypeStruct((4, BACK, D), bf16),
            jax.ShapeDtypeStruct((2, CHIPS, CHUNK, 16, 128), bf16),
        ),
        in_specs=[pl.BlockSpec(memory_space=VMEM)] * 11,
        out_specs=[pl.BlockSpec(memory_space=VMEM)] * 2,
        scratch_shapes=LOCAL_SCRATCH,
        compiler_params=pltpu.CompilerParams(vmem_limit_bytes=48 * 1024 * 1024),
        name="window_gradients",
    )(win, norm_gain.reshape(1, D), input_weight, output_weight, bias_table, regions, *consts)


def place():
    lon, lat = lax.axis_index("lon"), lax.axis_index("lat")
    x, z_hi, y, core = lon // 16, (lon // 8) % 2, (lon // 2) % 4, lon % 2
    return x, y, z_hi * 8 + lat, core


def at(x, y, z, core):
    return {"lon": ((x * 2 + z // 8) * 4 + y) * 2 + core, "lat": z % 8}


def window_owner(ha, ho, sign):
    lon, lat = lax.axis_index("lon"), lax.axis_index("lat")
    return {"lon": (lon + sign * ho + 64) % 64, "lat": (lat + sign * ha + 8) % 8}


def greet(partners):
    barrier = pltpu.get_barrier_semaphore()
    for partner in partners:
        pl.semaphore_signal(barrier, inc=1, device_id=partner, device_id_type=pl.DeviceIdType.MESH)
    pl.semaphore_wait(barrier, len(partners))


def remote(src, dst, send, recv, device):
    return pltpu.make_async_remote_copy(
        src_ref=src, dst_ref=dst, send_sem=send, recv_sem=recv, device_id=device,
        device_id_type=pl.DeviceIdType.MESH,
    )


QUADS = ((0, 0), (0, 1), (1, 0), (1, 1))


def halo_kernel(field_ref, cot_ref, out_ref, stage, send, land, send_sem, recv_sem):
    for quad, (ha, ho) in enumerate(QUADS):
        base = quad * SLOT
        stage[base + 2 * QUAD : base + SLOT, :] = jnp.zeros((SLOT - 2 * QUAD, D), f32)
        for which, ref in enumerate((field_ref, cot_ref)):
            for lev in range(2):
                for a in range(3):
                    row = base + which * QUAD + (lev * 3 + a) * 6
                    part = ref[1 - lev, a + 3 * (1 - ha)].astype(f32)
                    stage[row : row + 6, :] = part[6:12] if ho == 0 else part[0:6]
    send[...] = stage[...].astype(bf16).reshape(4, SLOT, D)
    greet([window_owner(ha, ho, sign) for ha, ho in QUADS[1:] for sign in (-1, 1)])
    copies = []
    for quad in (3, 1, 2):
        ha, ho = QUADS[quad]
        copies.append(
            remote(
                send.at[quad], land.at[quad], send_sem.at[quad], recv_sem.at[quad],
                window_owner(ha, ho, -1),
            )
        )
        copies[-1].start()
    out_ref[0] = send[0]
    for copy in copies:
        copy.wait_recv()
    for quad in range(1, 4):
        out_ref[quad] = land[quad]
    for copy in copies:
        copy.wait_send()


def halo_call(latent_field, cotangent):
    return pl.pallas_call(
        halo_kernel,
        out_shape=jax.ShapeDtypeStruct((4, SLOT, D), bf16),
        in_specs=[pl.BlockSpec(memory_space=VMEM)] * 2,
        out_specs=pl.BlockSpec(memory_space=VMEM),
        scratch_shapes=[
            VMEM((4 * SLOT, D), f32),
            VMEM((4, SLOT, D), bf16),
            VMEM((4, SLOT, D), bf16),
            pltpu.SemaphoreType.DMA((4,)),
            pltpu.SemaphoreType.DMA((4,)),
        ],
        compiler_params=pltpu.CompilerParams(
            collective_id=0, has_side_effects=True, vmem_limit_bytes=48 * 1024 * 1024
        ),
        name="halo",
    )(latent_field, cotangent)


def sums_kernel(
    back_ref, sums_ref, out_field, out_win, out_wout, out_gain, out_table,
    back_land, back_stage, pair, mine, chips, total, zland, owned, gathered, zhi_land, rows32, rows_send,
    rows_land, table, back_send_sem, back_recv_sem, pair_send, pair_recv, chip_send, chip_recv,
    z_send, z_recv, zg_send, zg_recv, hi_sem, tab_send, tab_recv, row_send, row_recv, last_sem,
):
    x, y, z, core = place()
    xy = x * 4 + y

    def shifted(k):
        return (x + k // 4) % 4, (y + k % 4) % 4

    def before(k):
        return (x - k // 4 + 4) % 4, (y - k % 4 + 4) % 4

    partners = [window_owner(ha, ho, sign) for ha, ho in QUADS[1:] for sign in (-1, 1)]
    partners.append(at(x, y, z, 1 - core))
    partners += [at(*shifted(k), z, core) for k in range(1, CHIPS)]
    partners += [at(x, y, (z + k) % 16, core) for k in range(1, 16)]
    greet(partners)

    order = list(range(1, CHIPS)) + [0]
    pairs = []
    for k in order:
        tx, ty = shifted(k)
        pairs.append(
            remote(
                sums_ref.at[1 - core, tx * 4 + ty], pair.at[k], pair_send.at[k], pair_recv.at[k],
                at(x, y, z, 1 - core),
            )
        )
        pairs[-1].start()
    backs = []
    for quad in (3, 1, 2):
        ha, ho = QUADS[quad]
        backs.append(
            remote(
                back_ref.at[quad], back_land.at[quad], back_send_sem.at[quad],
                back_recv_sem.at[quad], window_owner(ha, ho, 1),
            )
        )
        backs[-1].start()
    sends = []
    for k, copy in zip(order, pairs):
        copy.wait_recv()
        tx, ty = shifted(k)
        part = sums_ref[core, tx * 4 + ty].astype(f32) + pair[k].astype(f32)
        if k:
            mine[k] = part.astype(bf16)
            sends.append(
                remote(
                    mine.at[k], chips.at[k], chip_send.at[k], chip_recv.at[k], at(tx, ty, z, core)
                )
            )
            sends[-1].start()
        else:
            acc = part
    for k, copy in zip(order, sends):
        copy.wait_recv()
        acc = acc + chips[k].astype(f32)
    total[...] = acc.astype(bf16)

    gain_here = (core == GAIN_TILE // CORE_TILES) & (xy == GAIN_TILE % CORE_TILES)
    hi = remote(
        total.at[9], zhi_land, hi_sem.at[0], hi_sem.at[1], at(x, y, (z + 8) % 16, core)
    )
    hi.start()

    def to_owner(t):
        return remote(
            total.at[t], zland.at[(z - t + 16) % 16], z_send.at[t], z_recv.at[(z - t + 16) % 16],
            at(x, y, t, core),
        )

    for t in range(CHUNK):
        active = (z != t) if t < 9 else (z != t) & gain_here

        @pl.when(active)
        def _(t=t):
            to_owner(t).start()

    owner = (z < 9) | ((z == 9) & gain_here)

    def spread(k):
        return remote(
            owned, gathered.at[z], zg_send.at[k], zg_recv.at[z], at(x, y, (z + k) % 16, core)
        )

    @pl.when(owner)
    def _():
        acc = total[z].astype(f32)
        for k in range(1, 16):
            remote(total.at[0], zland.at[k], z_send.at[0], z_recv.at[k], at(x, y, z, core)).wait_recv()
            acc = acc + zland[k].astype(f32)
        owned[...] = acc.astype(bf16)
        for k in range(1, 16):
            spread(k).start()
        gathered[z] = owned[...]

    for t in range(CHUNK):
        active = (z != t) if t < 9 else (z != t) & gain_here

        @pl.when(active)
        def _(t=t):
            to_owner(t).wait_send()
            remote(
                owned, gathered.at[t], zg_send.at[0], zg_recv.at[t], at(x, y, z, core)
            ).wait_recv()

    hi.wait()
    tile = total[9].astype(f32) + zhi_land[...].astype(f32)
    summed = gathered[9].astype(f32)
    table[core * CORE_TILES + xy] = jnp.where(gain_here, summed, tile).astype(bf16)

    for t in range(9):
        rows32[(t % 3) * 16 : (t % 3) * 16 + 16, (t // 3) * 128 : (t // 3) * 128 + 128] = gathered[
            t
        ].astype(f32)
    z_hi = z // 8
    mine_z = rows32[pl.ds(pl.multiple_of(z_hi * 24, 8), 24), :]
    for to in range(4):
        part = mine_z[to * 6 : to * 6 + 6]
        rows_send[to] = jnp.concatenate([part, jnp.zeros((10, D), f32)], axis=0).astype(bf16)
    row_copies = []
    for k in range(1, 4):
        row_copies.append(
            remote(
                rows_send.at[(y + k) % 4], rows_land.at[y], row_send.at[k], row_recv.at[k],
                at(x, (y + k) % 4, z, core),
            )
        )
        row_copies[-1].start()
    slot = core * CORE_TILES + xy
    tab_copies = []
    for k in range(1, CHIPS):
        tab_copies.append(
            remote(
                table.at[slot], table.at[slot], tab_send.at[k], tab_recv.at[k],
                at(*shifted(k), z, core),
            )
        )
        tab_copies[-1].start()
    rows_land[y] = rows_send[y]
    for copy in backs:
        copy.wait_recv()
    for quad, (ha, ho) in enumerate(QUADS):
        block = (back_ref if quad == 0 else back_land)[quad].astype(f32)
        for lev in range(2):
            for a in range(3):
                row = (lev * 3 + a) * 6
                cell = ((1 - lev) * 6 + a + 3 * (1 - ha)) * 16 + 6 * (1 - ho)
                back_stage[cell : cell + 6, :] = block[row : row + 6]
    for lev in range(2):
        for a in range(6):
            cell = (lev * 6 + a) * 16
            out_field[lev, a] = back_stage[cell : cell + 16, :][:12].astype(bf16)
    for copy in tab_copies:
        copy.wait_recv()
    half = table.at[pl.ds(core * CORE_TILES, CORE_TILES)]
    last = remote(half, half, last_sem.at[0], last_sem.at[1], at(x, y, z, 1 - core))
    last.start()
    factor = 1.0 / math.sqrt(512 * CELLS)
    for copy in row_copies:
        copy.wait_recv()
    for b in range(4):
        rows = (rows_land[b].astype(f32) * factor)[:6].astype(bf16)
        if b < 3:
            out_win[:, b * D : (b + 1) * D] = rows
        else:
            out_wout[...] = rows
    last.wait_recv()
    for t in range(26):
        width = min(128, POS - t * 128)
        out_table[0, :, t * 128 : t * 128 + width] = table[t].astype(f32)[:HEADS, :width]
    gains = table[GAIN_TILE].astype(f32) * factor
    for k in range(3):
        out_gain[:, k * 128 : k * 128 + 128] = gains[k : k + 1]
    for copy in pairs + backs + sends + row_copies + tab_copies + [last]:
        copy.wait_send()

    @pl.when(owner)
    def _():
        for k in range(1, 16):
            spread(k).wait_send()


def sums_call(back, sums):
    tile = (16, 128)
    sem = pltpu.SemaphoreType.DMA
    return pl.pallas_call(
        sums_kernel,
        out_shape=(
            jax.ShapeDtypeStruct((LEV, WIN_LAT, WIN_LON, D), bf16),
            jax.ShapeDtypeStruct((6, 3 * D), bf16),
            jax.ShapeDtypeStruct((6, D), bf16),
            jax.ShapeDtypeStruct((1, D), f32),
            jax.ShapeDtypeStruct((1, HEADS, POS), f32),
        ),
        in_specs=[pl.BlockSpec(memory_space=VMEM)] * 2,
        out_specs=[pl.BlockSpec(memory_space=VMEM)] * 5,
        scratch_shapes=[
            VMEM((4, BACK, D), bf16),
            VMEM((ROWS * 16, D), f32),
            VMEM((CHIPS, CHUNK) + tile, bf16),
            VMEM((CHIPS, CHUNK) + tile, bf16),
            VMEM((CHIPS, CHUNK) + tile, bf16),
            VMEM((CHUNK,) + tile, bf16),
            VMEM((16,) + tile, bf16),
            VMEM(tile, bf16),
            VMEM((16,) + tile, bf16),
            VMEM(tile, bf16),
            VMEM((48, D), f32),
            VMEM((4, 16, D), bf16),
            VMEM((4, 16, D), bf16),
            VMEM((32,) + tile, bf16),
            sem((4,)), sem((4,)), sem((CHIPS,)), sem((CHIPS,)), sem((CHIPS,)), sem((CHIPS,)),
            sem((CHUNK,)), sem((16,)), sem((16,)), sem((16,)), sem((2,)), sem((CHIPS,)),
            sem((CHIPS,)), sem((4,)), sem((4,)), sem((2,)),
        ],
        compiler_params=pltpu.CompilerParams(
            collective_id=1, has_side_effects=True, vmem_limit_bytes=48 * 1024 * 1024
        ),
        name="sums",
    )(back, sums)


def on_device(latent_field, cotangent, norm_gain, input_weight, output_weight, bias_table, regions):
    win = halo_call(latent_field, cotangent)
    back, sums = local_call(win, norm_gain, input_weight, output_weight, bias_table, regions)
    field, grad_in, grad_out, gain, table = sums_call(back, sums)
    return field, grad_in, grad_out, gain.reshape(D), table


def solution(mesh):
    in_specs = (
        P(None, "lat", "lon", None),
        P(None, "lat", "lon", None),
        P(),
        P(),
        P(),
        P("lat", None, None),
        P(None, "lat", "lon"),
    )
    out_specs = (
        P(None, "lat", "lon", None),
        P("lon", None),
        P("lon", None),
        P(),
        P("lat", None, None),
    )
    return jax.shard_map(
        on_device, mesh=mesh, in_specs=in_specs, out_specs=out_specs, check_vma=False
    )
```

```python
import functools
import math

import jax
import jax.numpy as jnp
import numpy as np
from jax import lax
from jax.experimental import pallas as pl
from jax.experimental.pallas import tpu as pltpu
from jax.sharding import PartitionSpec as P

D = 384
HEADS = 12
HEAD_DIM = 32
LEV = 2
WIN_LAT = 6
WIN_LON = 12
CELLS = 144
ROWS = LEV * WIN_LAT
SPREAD = 2 * WIN_LON - 1
HALF_POS = WIN_LAT * SPREAD
POS = 3312
WIDE = 256
CHIPS = 16
TOKENS = 512 * CELLS
TABLE_TILES = 26
GROUPS = 3
KEEP = 80
SCATTER = WIN_LON * ROWS * 16

norm_eps = 1e-05
masked_score = -1000000000.0
VMEM = pltpu.VMEM
f32 = jnp.float32
bf16 = jnp.bfloat16


def feature_order():
    out = np.zeros((2, 512, D), np.float32)
    for core in range(2):
        for x in range(4):
            for y in range(4):
                for z_hi in range(2):
                    lon = ((x * 2 + z_hi) * 4 + y) * 2 + core
                    for k in range(6):
                        row = ((core * 4 + x) * 4 + y) * 16 + z_hi * 6 + k
                        out[0, row, lon * 6 + k] = 1
                        out[1, row + 4, lon * 6 + k] = 1
    return out


def bias_selectors():
    out = np.zeros((WIN_LON, 2 * HALF_POS, WIDE), np.float32)
    for c in range(WIN_LON):
        for p in range(CELLS):
            d, v, lev = p // ROWS, (p % ROWS) // 2, 1 - p % 2
            out[c, lev * HALF_POS + v * SPREAD + c - d + WIN_LON - 1, p] = 1
    return out


def table_offset(row, y):
    x, u = 1 - row % 2, row // 2
    return ((x * 2 + y) * WIN_LAT + u) * HALF_POS


def head_rows(ref, h):
    return jnp.concatenate(
        [ref[pl.ds(half * SCATTER + h, CELLS, stride=16), :] for half in range(2)], axis=1
    )


def put_head_rows(ref, h, value):
    for half in range(2):
        ref[pl.ds(half * SCATTER + h, CELLS, stride=16), :] = value[:, half * 128 : half * 128 + 128]


def nt(a, b):
    return lax.dot_general(a, b, (((1,), (1,)), ((), ())), preferred_element_type=f32)


def nn(a, b):
    return lax.dot_general(a, b, (((1,), (0,)), ((), ())), preferred_element_type=f32)


def tn(a, b):
    return lax.dot_general(a, b, (((0,), (0,)), ((), ())), preferred_element_type=f32)


def iota(shape, dim):
    return lax.broadcasted_iota(jnp.int32, shape, dim)


def place():
    lon, lat = lax.axis_index("lon"), lax.axis_index("lat")
    x, z_hi, y, core = lon // 16, (lon // 8) % 2, (lon // 2) % 4, lon % 2
    return x, y, z_hi * 8 + lat, core


def at(x, y, z, core):
    return {"lon": ((x * 2 + z // 8) * 4 + y) * 2 + core, "lat": z % 8}


def window_owner(ha, ho, sign):
    lon, lat = lax.axis_index("lon"), lax.axis_index("lat")
    return {"lon": (lon + sign * ho + 64) % 64, "lat": (lat + sign * ha + 8) % 8}


def greet(partners):
    barrier = pltpu.get_barrier_semaphore()
    for partner in partners:
        pl.semaphore_signal(barrier, inc=1, device_id=partner, device_id_type=pl.DeviceIdType.MESH)
    return len(partners)


def greeted(count):
    pl.semaphore_wait(pltpu.get_barrier_semaphore(), count)


def remote(src, dst, send, recv, device):
    return pltpu.make_async_remote_copy(
        src_ref=src, dst_ref=dst, send_sem=send, recv_sem=recv, device_id=device,
        device_id_type=pl.DeviceIdType.MESH,
    )


QUADS = ((0, 0), (0, 1), (1, 0), (1, 1))


def cells_part(ref, ha, ho):
    return ref.at[pl.ds(3 * (1 - ha), 3), pl.ds(6 * (1 - ho), 6)]


def window_part(ref, ha, ho):
    return ref.at[pl.ds(3 * ha, 3), pl.ds(6 * ho, 6)]


def halo_partners():
    return [window_owner(ha, ho, sign) for ha, ho in QUADS[1:] for sign in (-1, 1)]


def expand_table(table, sel_ref, tprime, bias):
    table = table[0].astype(f32)
    tprime[...] = jnp.zeros_like(tprime)
    for row in range(ROWS):
        for y in range(2):
            off = table_offset(row, y)
            tprime[row * 16 : row * 16 + HEADS, y * HALF_POS : (y + 1) * HALF_POS] = table[
                :, off : off + HALF_POS
            ]
    rows = tprime[...].astype(bf16)
    for c in range(WIN_LON):
        part = nn(rows, sel_ref[c])
        for half in range(2):
            base = half * SCATTER + c * 192
            bias[base : base + 192, :] = part[:, half * 128 : half * 128 + 128]


def same_region(reg, regs):
    for a in range(WIN_LAT):
        for lev in range(2):
            regs[a * 2 + lev : a * 2 + lev + 1, 0:WIN_LON] = reg[a, 1 - lev : 2 - lev].astype(f32)
    grid = regs[0:ROWS, 0:WIN_LON].astype(bf16)
    where = iota((ROWS, WIDE), 1)
    spread = nn(grid, (where // ROWS == iota((ROWS, WIDE), 0)).astype(bf16))
    row = jnp.sum(
        jnp.where(where % ROWS == iota((ROWS, WIDE), 0), spread, 0.0), axis=0, keepdims=True
    )
    kind = iota((16, WIDE), 0).astype(f32)
    hot = jnp.where((row == kind) & (iota((16, WIDE), 1) < CELLS), 1.0, 0.0)
    return tn(hot[:, :CELLS].astype(bf16), hot.astype(bf16))


def cells_to_rows(land, stage):
    for a in range(WIN_LAT):
        for o in range(WIN_LON):
            p = o * ROWS + a * 2
            stage[p : p + 2, :] = land[a, o].astype(f32)


def pad_cells(a):
    return jnp.concatenate([a, jnp.zeros((WIDE - CELLS, a.shape[1]), a.dtype)], axis=0)


def keep_rows():
    shape = (2 * KEEP, CELLS + 16)
    row, col = iota(shape, 0), iota(shape, 1)
    half, w = row // KEEP, row % KEEP
    own = (w // 6) * 12 + half * 6 + w % 6
    gain = CELLS + HEADS + jnp.minimum(w - 72, 3)
    return (col == jnp.where(w < 72, own, gain)).astype(bf16)


FAR_FIRST = (10, 6, 9, 11, 14, 2, 8, 5, 7, 13, 15, 1, 3, 4, 12)


def window_kernel(
    field_hbm, cot_hbm, gain_hbm, win_hbm, wout_hbm, table_hbm, reg_hbm, sel_hbm, feat_hbm,
    field_out, rows_out, table_out,
    field_land, cot_land, gain_v, w_in, w_out, table, reg, sel, feat, tprime, regs, stage,
    qkv, normt, bias, probs, dsf, dpt, att, tabf, grad_rows, gwin,
    sums, pair, mine, chips, tsums, tpair, tmine, tchips, plane_sums, pack, pack_land, owned, zland,
    hi_land,
    load_sem, own_sem, halo_send, halo_recv, back_send, back_recv, core_send, core_recv, chip_send,
    chip_recv, z_send, z_recv, zp_sem, hi_sem, tab_send, tab_recv, last_sem,
):
    x, y, z, core = place()
    xy = x * 4 + y
    z_hi, parity = z // 8, z % 2
    z_pair = z + 1 - 2 * parity
    other_core = at(x, y, z, 1 - core)

    def plane(k):
        tx, ty = (x + k // 4) % 4, (y + k % 4) % 4
        return tx * 4 + ty, at(tx, ty, z, core)

    partners = halo_partners() + [other_core]
    partners += [plane(k)[1] for k in range(1, CHIPS)]
    partners += [at(x, y, (z + k) % 16, core) for k in range(1, 16)]
    count = greet(partners)
    owns = [
        pltpu.make_async_copy(cells_part(src, 0, 0), window_part(dst, 0, 0), own_sem.at[i])
        for i, (src, dst) in enumerate(((field_hbm, field_land), (cot_hbm, cot_land)))
    ]
    loads = [
        pltpu.make_async_copy(src, dst, load_sem.at[i])
        for i, (src, dst) in enumerate(
            (
                (table_hbm, table), (sel_hbm, sel), (reg_hbm, reg), (gain_hbm, gain_v),
                (win_hbm, w_in), (feat_hbm, feat), (wout_hbm, w_out),
            )
        )
    ]
    for copy in loads + owns:
        copy.start()
    greeted(count)

    halos = [[], []]
    for i, (src, dst) in enumerate(((field_hbm, field_land), (cot_hbm, cot_land))):
        for quad in (3, 1, 2):
            ha, ho = QUADS[quad]
            halos[i].append(
                remote(
                    cells_part(src, ha, ho), window_part(dst, ha, ho), halo_send.at[i, quad],
                    halo_recv.at[i, quad], window_owner(ha, ho, -1),
                )
            )
            halos[i][-1].start()
    for copy in loads:
        copy.wait()
    same = same_region(reg, regs) > 0.5
    expand_table(table, sel, tprime, bias)

    owns[0].wait()
    for copy in halos[0]:
        copy.wait_recv()
    cells_to_rows(field_land, stage)
    cells = stage[...]
    centred = cells - jnp.mean(cells, axis=1, keepdims=True)
    inv_std = lax.rsqrt(jnp.mean(centred * centred, axis=1, keepdims=True) + norm_eps)
    normalized = centred * inv_std
    stage[...] = normalized
    gain = gain_v[...].reshape(1, D)
    normed = (normalized * gain).astype(bf16)
    qkv[:, : 3 * D] = nn(normed, w_in[...]).astype(bf16)
    for i in range(2):
        normt[i] = nt(feat[i], normed).astype(bf16)

    scale = HEAD_DIM ** -0.5
    eye = (iota((128, 128), 0) == iota((128, 128), 1)).astype(bf16)
    lane = iota((CELLS, 128), 1) // HEAD_DIM
    zero = jnp.zeros((CELLS, 128), bf16)

    def part(which, g):
        lo = which * D + g * 128
        return qkv[:, lo : lo + 128]

    def four_heads(a):
        return jnp.concatenate([jnp.where(lane == e, a, zero) for e in range(4)], axis=0)

    for g in range(GROUPS):
        q, k, v = part(0, g), pad_cells(part(1, g)), pad_cells(part(2, g))
        v_t = nt(eye, v).astype(bf16)
        scores = nt(four_heads(q), k)
        for e in range(4):
            h = g * 4 + e
            r = e * HEAD_DIM
            s = scores[e * CELLS : (e + 1) * CELLS] * scale + head_rows(bias, h)
            s = jnp.where(same, s, masked_score)
            s = jnp.exp(s - jnp.max(s, axis=1, keepdims=True))
            p = s * (1.0 / jnp.sum(s, axis=1, keepdims=True))
            probs[h] = p
            att[h * 32 : h * 32 + 32, :] = nt(v_t[r : r + 32], p.astype(bf16)).astype(bf16)
    att_t = nn(feat[1], att[...]).astype(bf16)

    owns[1].wait()
    for copy in halos[1]:
        copy.wait_recv()
    cells_to_rows(cot_land, grad_rows)
    cot = grad_rows[...].astype(bf16)
    qkv[:, 3 * D :] = nt(cot, w_out[...]).astype(bf16)

    core_copies = [
        remote(sums.at[g, 1 - core], pair.at[g], core_send.at[g], core_recv.at[g], other_core)
        for g in range(GROUPS)
    ]
    core_copies.append(
        remote(tsums.at[1 - core], tpair, core_send.at[3], core_recv.at[3], other_core)
    )
    sends = [[], [], [], []]

    def to_plane(g):
        core_copies[g].wait_recv()
        if g < GROUPS:
            mine[g] = (sums[g, core].astype(f32) + pair[g].astype(f32)).astype(bf16)
        else:
            tmine[...] = (tsums[core].astype(f32) + tpair[...].astype(f32)).astype(bf16)
        for k in FAR_FIRST:
            index, device = plane(k)
            src, dst = (
                (mine.at[g, index], chips.at[g, k])
                if g < GROUPS
                else (tmine.at[index], tchips.at[k])
            )
            sends[g].append(remote(src, dst, chip_send.at[g, k], chip_recv.at[g, k], device))
            sends[g][-1].start()

    for g in range(GROUPS):
        q, k, v, do = part(0, g), pad_cells(part(1, g)), pad_cells(part(2, g)), part(3, g)
        q_t = nt(eye, q).astype(bf16)
        k_t = nt(eye, k).astype(bf16)
        do_t = nt(eye, do).astype(bf16)
        grad_probs = nt(four_heads(do), v)
        for e in range(4):
            h = g * 4 + e
            r = e * HEAD_DIM
            p = probs[h]
            dp = grad_probs[e * CELLS : (e + 1) * CELLS]
            dpt[2 * D + h * 32 : 2 * D + h * 32 + 32, :] = nn(do_t[r : r + 32], p.astype(bf16))[
                :, :CELLS
            ].astype(bf16)
            ds = p * (dp - jnp.sum(p * dp, axis=1, keepdims=True))
            put_head_rows(dsf, h, ds)
            ds_low = (ds * scale).astype(bf16)
            dpt[h * 32 : h * 32 + 32, :] = nt(k_t[r : r + 32], ds_low).astype(bf16)
            dpt[D + h * 32 : D + h * 32 + 32, :] = nn(q_t[r : r + 32], ds_low)[:, :CELLS].astype(
                bf16
            )
        blocks = [
            nt(normt[which % 2], dpt[which * D + g * 128 : which * D + g * 128 + 128, :])
            for which in range(3)
        ]
        blocks.append(nn(att_t, cot[:, g * 128 : g * 128 + 128]))
        b0, b1, b2, b3 = (b.reshape(32, 2, 8, 128) for b in blocks)
        sums[g] = (
            jnp.concatenate(
                [b0[:, 0], b0[:, 1] + b1[:, 0], b1[:, 1], b2[:, 0], b2[:, 1] + b3[:, 0], b3[:, 1]],
                axis=1,
            )
            .astype(bf16)
            .reshape(2, CHIPS, 48, 128)
        )
        core_copies[g].start()
        if g:
            to_plane(g - 1)

    shifted_t = nn(w_in[...], dpt[...]).astype(bf16)
    eye_c = (iota((CELLS, CELLS), 0) == iota((CELLS, CELLS), 1)).astype(bf16)
    g_normed = nt(eye_c, shifted_t)
    normalized = stage[...]
    scaled = g_normed * gain
    grad_gain = jnp.sum(g_normed * normalized, axis=0, keepdims=True)
    grad_rows[...] = cot.astype(f32) + inv_std * (
        scaled
        - jnp.mean(scaled, axis=1, keepdims=True)
        - normalized * jnp.mean(scaled * normalized, axis=1, keepdims=True)
    )
    for a in range(WIN_LAT):
        for o in range(WIN_LON):
            p = o * ROWS + a * 2
            gwin[a, o] = grad_rows[p : p + 2, :].astype(bf16)
    backs = []
    for quad in (3, 1, 2):
        ha, ho = QUADS[quad]
        backs.append(
            remote(
                window_part(gwin, ha, ho), cells_part(field_out, ha, ho), back_send.at[quad],
                back_recv.at[quad], window_owner(ha, ho, 1),
            )
        )
        backs[-1].start()
    to_plane(2)

    for h in range(HEADS, 16):
        put_head_rows(dsf, h, jnp.zeros((CELLS, WIDE), f32))
    acc = jnp.zeros((192, 2 * HALF_POS), f32)
    for c in range(WIN_LON):
        rows = jnp.concatenate(
            [dsf[pl.ds(half * SCATTER + c * 192, 192), :] for half in range(2)], axis=1
        )
        acc = acc + nt(rows.astype(bf16), sel[c])
    tabf[:, 25 * 128 : 32 * 128] = jnp.zeros((16, 7 * 128), f32)
    for row in range(ROWS):
        for half in range(2):
            off = table_offset(row, half)
            tabf[:, off : off + HALF_POS] = acc[
                row * 16 : row * 16 + 16, half * HALF_POS : (half + 1) * HALF_POS
            ]
    spare = jnp.concatenate(
        [grad_gain[:, k * 128 : k * 128 + 128] for k in range(3)] + [jnp.zeros((1, 128), f32)],
        axis=0,
    )
    for t in range(32):
        tsums[t // 16, t % 16] = jnp.concatenate(
            [tabf[0:HEADS, t * 128 : t * 128 + 128], spare], axis=0
        ).astype(bf16)
    core_copies[3].start()
    for a in range(3):
        for o in range(6):
            field_out[3 + a, 6 + o] = gwin[a, o]
    to_plane(3)

    for g in range(GROUPS):
        for copy in sends[g]:
            copy.wait_recv()
        acc = mine[g, xy].astype(f32)
        for k in range(1, CHIPS):
            acc = acc + chips[g, k].astype(f32)
        plane_sums[g * 48 : (g + 1) * 48, :] = acc.astype(bf16)
    for copy in sends[3]:
        copy.wait_recv()
    acc = tmine[xy].astype(f32)
    for k in range(1, CHIPS):
        acc = acc + tchips[k].astype(f32)
    plane_sums[CELLS : CELLS + 16, :] = acc.astype(bf16)

    pack[...] = nn(keep_rows(), plane_sums[...]).astype(bf16).reshape(2, KEEP, 128)
    swap = remote(
        pack.at[1 - parity], pack_land, zp_sem.at[0], zp_sem.at[1], at(x, y, z_pair, core)
    )
    swap.start()
    table_part = plane_sums.at[pl.ds(CELLS, 16)]
    hi = remote(table_part, hi_land, hi_sem.at[0], hi_sem.at[1], at(x, y, (z + 8) % 16, core))
    hi.start()
    swap.wait_recv()
    owned[...] = (pack[parity].astype(f32) + pack_land[...].astype(f32)).astype(bf16)

    def keeper(j):
        return parity * 8 + (z + 4 + j) % 8

    def to_keeper(j):
        return remote(
            owned, zland.at[z // 2], z_send.at[j], z_recv.at[z // 2], at(x, y, keeper(j), core)
        )

    for j in range(8):

        @pl.when(keeper(j) != z)
        def _(j=j):
            to_keeper(j).start()

    @pl.when(parity == z_hi)
    def _():
        zland[z // 2] = owned[...]

    hi.wait_recv()
    slot = core * CHIPS + xy
    table_out[slot] = (plane_sums[CELLS : CELLS + 16].astype(f32) + hi_land[...].astype(f32)).astype(
        bf16
    )
    tab_copies = []
    for k in FAR_FIRST:
        tab_copies.append(
            remote(
                table_out.at[slot], table_out.at[slot], tab_send.at[k], tab_recv.at[k], plane(k)[1]
            )
        )
        tab_copies[-1].start()

    for i in range(8):

        @pl.when(2 * i + z_hi != z)
        def _(i=i):
            remote(
                owned, zland.at[i], z_send.at[0], z_recv.at[i], at(x, y, z_pair, core)
            ).wait_recv()

    total = zland[0].astype(f32)
    for i in range(1, 8):
        total = total + zland[i].astype(f32)
    rows_out[...] = total

    for copy in tab_copies:
        copy.wait_recv()
    half = table_out.at[pl.ds(core * CHIPS, CHIPS)]
    last = remote(half, half, last_sem.at[0], last_sem.at[1], other_core)
    last.start()
    for copy in backs + [last]:
        copy.wait_recv()
    for copy in halos[0] + halos[1] + core_copies + sum(sends, []) + backs + [swap, hi, last]:
        copy.wait_send()
    for copy in tab_copies:
        copy.wait_send()
    for j in range(8):

        @pl.when(keeper(j) != z)
        def _(j=j):
            to_keeper(j).wait_send()


def window_call(*args):
    tile = (16, 128)
    grid = (WIN_LAT, WIN_LON, LEV, D)
    sem = pltpu.SemaphoreType.DMA
    return pl.pallas_call(
        window_kernel,
        out_shape=(
            jax.ShapeDtypeStruct(grid, bf16),
            jax.ShapeDtypeStruct((KEEP, 128), f32),
            jax.ShapeDtypeStruct((32,) + tile, bf16),
        ),
        in_specs=[pl.BlockSpec(memory_space=pl.ANY)] * 9,
        out_specs=[pl.BlockSpec(memory_space=VMEM)] * 3,
        scratch_shapes=[
            VMEM(grid, bf16),
            VMEM(grid, bf16),
            VMEM((D,), f32),
            VMEM((D, 3 * D), bf16),
            VMEM((D, D), bf16),
            VMEM((1, HEADS, POS), bf16),
            VMEM((WIN_LAT, LEV, WIN_LON), jnp.int32),
            VMEM((WIN_LON, 2 * HALF_POS, WIDE), bf16),
            VMEM((2, 512, D), bf16),
            VMEM((192, 2 * HALF_POS), f32),
            VMEM((16, 128), f32),
            VMEM((CELLS, D), f32),
            VMEM((CELLS, 4 * D), bf16),
            VMEM((2, 512, CELLS), bf16),
            VMEM((2 * SCATTER, 128), f32),
            VMEM((HEADS, CELLS, WIDE), f32),
            VMEM((2 * SCATTER, 128), f32),
            VMEM((3 * D, CELLS), bf16),
            VMEM((D, CELLS), bf16),
            VMEM((16, 32 * 128), f32),
            VMEM((CELLS, D), f32),
            VMEM(grid, bf16),
            VMEM((GROUPS, 2, CHIPS, 48, 128), bf16),
            VMEM((GROUPS, CHIPS, 48, 128), bf16),
            VMEM((GROUPS, CHIPS, 48, 128), bf16),
            VMEM((GROUPS, CHIPS, 48, 128), bf16),
            VMEM((2, CHIPS) + tile, bf16),
            VMEM((CHIPS,) + tile, bf16),
            VMEM((CHIPS,) + tile, bf16),
            VMEM((CHIPS,) + tile, bf16),
            VMEM((CELLS + 16, 128), bf16),
            VMEM((2, KEEP, 128), bf16),
            VMEM((KEEP, 128), bf16),
            VMEM((KEEP, 128), bf16),
            VMEM((8, KEEP, 128), bf16),
            VMEM(tile, bf16),
            sem((7,)), sem((2,)), sem((2, 4)), sem((2, 4)), sem((4,)), sem((4,)), sem((4,)),
            sem((4,)), sem((4, CHIPS)), sem((4, CHIPS)), sem((8,)), sem((8,)), sem((2,)),
            sem((2,)), sem((CHIPS,)), sem((CHIPS,)), sem((2,)),
        ],
        compiler_params=pltpu.CompilerParams(
            collective_id=0, has_side_effects=True, vmem_limit_bytes=60 * 1024 * 1024
        ),
        name="window_gradients",
    )(*args)


def finish_kernel(field, rows, table, out_field, out_win, out_wout, out_gain, out_table):
    factor = 1.0 / math.sqrt(TOKENS)
    out_field[...] = field[...]
    sums = rows[...] * factor
    for g in range(GROUPS):
        for which in range(4):
            at_row = (g * 4 + which) * 6
            part = sums[at_row : at_row + 6].astype(bf16)
            if which < 3:
                lo = which * D + g * 128
                out_win[:, lo : lo + 128] = part
            else:
                out_wout[:, g * 128 : g * 128 + 128] = part
    for k in range(3):
        out_gain[k * 128 : k * 128 + 128] = sums[72 + k]
    for t in range(TABLE_TILES):
        width = min(128, POS - t * 128)
        values = table[t].astype(f32)
        for h in range(HEADS):
            out_table[h, :, t * 128 : t * 128 + width] = values[h : h + 1, :width]


def finish_call(field, rows, table):
    return pl.pallas_call(
        finish_kernel,
        out_shape=(
            jax.ShapeDtypeStruct((WIN_LAT, WIN_LON, LEV, D), bf16),
            jax.ShapeDtypeStruct((6, 3 * D), bf16),
            jax.ShapeDtypeStruct((6, D), bf16),
            jax.ShapeDtypeStruct((D,), f32),
            jax.ShapeDtypeStruct((HEADS, 1, POS), f32),
        ),
        in_specs=[pl.BlockSpec(memory_space=VMEM)] * 3,
        out_specs=[pl.BlockSpec(memory_space=VMEM)] * 5,
        compiler_params=pltpu.CompilerParams(vmem_limit_bytes=60 * 1024 * 1024),
        name="outputs",
    )(field, rows, table)


def on_device(latent_field, cotangent, norm_gain, input_weight, output_weight, bias_table, regions):
    sel = jnp.asarray(bias_selectors(), bf16)
    feat = jnp.asarray(feature_order(), bf16)
    field, cot = (jnp.transpose(a, (1, 2, 0, 3)) for a in (latent_field, cotangent))
    reg = jnp.transpose(regions, (1, 0, 2))
    sums = window_call(
        field, cot, norm_gain, input_weight, output_weight, bias_table, reg, sel, feat
    )
    grad_field, grad_in, grad_out, grad_gain, table = finish_call(*sums)
    return (
        jnp.transpose(grad_field, (2, 0, 1, 3)),
        grad_in,
        grad_out,
        grad_gain,
        jnp.transpose(table, (1, 0, 2)),
    )


def solution(mesh):
    in_specs = (
        P(None, "lat", "lon", None),
        P(None, "lat", "lon", None),
        P(),
        P(),
        P(),
        P("lat", None, None),
        P(None, "lat", "lon"),
    )
    out_specs = (
        P(None, "lat", "lon", None),
        P("lon", None),
        P("lon", None),
        P(),
        P("lat", None, None),
    )
    return jax.shard_map(
        on_device, mesh=mesh, in_specs=in_specs, out_specs=out_specs, check_vma=False
    )
```

```python
import functools
import math

import jax
import jax.numpy as jnp
import numpy as np
from jax import lax
from jax.experimental import pallas as pl
from jax.experimental.pallas import tpu as pltpu
from jax.sharding import PartitionSpec as P

D = 384
HEADS = 12
HEAD_DIM = 32
LEV = 2
WIN_LAT = 6
WIN_LON = 12
CELLS = 144
ROWS = LEV * WIN_LAT
SPREAD = 2 * WIN_LON - 1
HALF_POS = WIN_LAT * SPREAD
POS = 3312
WIDE = 256
CHIPS = 16
TOKENS = 512 * CELLS
TABLE_TILES = 26
GROUPS = 3
KEEP = (32, 16)
SCATTER = WIN_LON * ROWS * 16

norm_eps = 1e-05
masked_score = -1000000000.0
VMEM = pltpu.VMEM
f32 = jnp.float32
bf16 = jnp.bfloat16


def feature_order():
    out = np.zeros((2, 512, D), np.float32)
    for core in range(2):
        for x in range(4):
            for y in range(4):
                for z_hi in range(2):
                    lon = ((x * 2 + z_hi) * 4 + y) * 2 + core
                    for k in range(6):
                        row = ((core * 4 + x) * 4 + y) * 16 + z_hi * 6 + k
                        out[0, row, lon * 6 + k] = 1
                        out[1, row + 4, lon * 6 + k] = 1
    return out


def bias_selectors():
    out = np.zeros((WIN_LON, 2 * HALF_POS, WIDE), np.float32)
    for c in range(WIN_LON):
        for p in range(CELLS):
            d, v, lev = p // ROWS, (p % ROWS) // 2, 1 - p % 2
            out[c, lev * HALF_POS + v * SPREAD + c - d + WIN_LON - 1, p] = 1
    return out


def table_offset(row, y):
    x, u = 1 - row % 2, row // 2
    return ((x * 2 + y) * WIN_LAT + u) * HALF_POS


def head_rows(ref, h):
    return jnp.concatenate(
        [ref[pl.ds(half * SCATTER + h, CELLS, stride=16), :] for half in range(2)], axis=1
    )


def put_head_rows(ref, h, value):
    for half in range(2):
        ref[pl.ds(half * SCATTER + h, CELLS, stride=16), :] = value[:, half * 128 : half * 128 + 128]


def nt(a, b):
    return lax.dot_general(a, b, (((1,), (1,)), ((), ())), preferred_element_type=f32)


def nn(a, b):
    return lax.dot_general(a, b, (((1,), (0,)), ((), ())), preferred_element_type=f32)


def tn(a, b):
    return lax.dot_general(a, b, (((0,), (0,)), ((), ())), preferred_element_type=f32)


def iota(shape, dim):
    return lax.broadcasted_iota(jnp.int32, shape, dim)


def place():
    lon, lat = lax.axis_index("lon"), lax.axis_index("lat")
    x, z_hi, y, core = lon // 16, (lon // 8) % 2, (lon // 2) % 4, lon % 2
    return x, y, z_hi * 8 + lat, core


def at(x, y, z, core):
    return {"lon": ((x * 2 + z // 8) * 4 + y) * 2 + core, "lat": z % 8}


def window_owner(ha, ho, sign):
    lon, lat = lax.axis_index("lon"), lax.axis_index("lat")
    return {"lon": (lon + sign * ho + 64) % 64, "lat": (lat + sign * ha + 8) % 8}


def greet(partners):
    barrier = pltpu.get_barrier_semaphore()
    for partner in partners:
        pl.semaphore_signal(barrier, inc=1, device_id=partner, device_id_type=pl.DeviceIdType.MESH)
    return len(partners)


def greeted(count):
    pl.semaphore_wait(pltpu.get_barrier_semaphore(), count)


def remote(src, dst, send, recv, device):
    return pltpu.make_async_remote_copy(
        src_ref=src, dst_ref=dst, send_sem=send, recv_sem=recv, device_id=device,
        device_id_type=pl.DeviceIdType.MESH,
    )


QUADS = ((0, 0), (0, 1), (1, 0), (1, 1))


def cells_part(ref, ha, ho):
    return ref.at[pl.ds(3 * (1 - ha), 3), pl.ds(6 * (1 - ho), 6)]


def window_part(ref, ha, ho):
    return ref.at[pl.ds(3 * ha, 3), pl.ds(6 * ho, 6)]


def halo_partners():
    return [window_owner(ha, ho, sign) for ha, ho in QUADS[1:] for sign in (-1, 1)]


def expand_table(table, sel_ref, tprime, bias):
    table = table[0].astype(f32)
    tprime[...] = jnp.zeros_like(tprime)
    for row in range(ROWS):
        for y in range(2):
            off = table_offset(row, y)
            tprime[row * 16 : row * 16 + HEADS, y * HALF_POS : (y + 1) * HALF_POS] = table[
                :, off : off + HALF_POS
            ]
    rows = tprime[...].astype(bf16)
    for c in range(WIN_LON):
        part = nn(rows, sel_ref[c])
        for half in range(2):
            base = half * SCATTER + c * 192
            bias[base : base + 192, :] = part[:, half * 128 : half * 128 + 128]


def same_region(reg, regs):
    for a in range(WIN_LAT):
        for lev in range(2):
            regs[a * 2 + lev : a * 2 + lev + 1, 0:WIN_LON] = reg[a, 1 - lev : 2 - lev].astype(f32)
    grid = regs[0:ROWS, 0:WIN_LON].astype(bf16)
    where = iota((ROWS, WIDE), 1)
    spread = nn(grid, (where // ROWS == iota((ROWS, WIDE), 0)).astype(bf16))
    row = jnp.sum(
        jnp.where(where % ROWS == iota((ROWS, WIDE), 0), spread, 0.0), axis=0, keepdims=True
    )
    kind = iota((16, WIDE), 0).astype(f32)
    hot = jnp.where((row == kind) & (iota((16, WIDE), 1) < CELLS), 1.0, 0.0)
    return tn(hot[:, :CELLS].astype(bf16), hot.astype(bf16))


def cells_to_rows(land, stage):
    for a in range(WIN_LAT):
        for o in range(WIN_LON):
            p = o * ROWS + a * 2
            stage[p : p + 2, :] = land[a, o].astype(f32)


def pad_cells(a):
    return jnp.concatenate([a, jnp.zeros((WIDE - CELLS, a.shape[1]), a.dtype)], axis=0)


def keep_rows(pieces, rows):
    shape = (4 * rows, pieces * 12 + (16 if pieces == 4 else 0))
    row, col = iota(shape, 0), iota(shape, 1)
    part, w = row // rows, row % rows
    mine = pieces // 2 * 6
    own = ((part % 2) * (pieces // 2) + w // 6) * 12 + (part // 2) * 6 + w % 6
    gain = jnp.where((part % 2 == 0) & (w < mine + 3), pieces * 12 + w - mine, -1)
    return (col == jnp.where(w < mine, own, gain if pieces == 4 else -1)).astype(bf16)


FAR_FIRST = (10, 6, 9, 11, 14, 2, 8, 5, 7, 13, 15, 1, 3, 4, 12)


def window_kernel(
    field_hbm, cot_hbm, gain_hbm, win_hbm, wout_hbm, table_hbm, reg_hbm, sel_hbm, feat_hbm,
    field_out, rows_out, table_out,
    field_land, cot_land, gain_v, w_in, w_out, table, reg, sel, feat, tprime, regs, stage,
    qkv, normt, bias, probs, dsf, dpt, att, tabf, grad_rows, gwin,
    sums, pair, mine, chips, last_sums, last_pair, last_mine, last_chips, tsums, tpair, tmine, tchips,
    pack, pack_land, owned, zland, last_pack, last_pack_land, last_owned, last_zland, hi_send, hi_land,
    ds_s,
    load_sem, own_sem, halo_send, halo_recv, back_send, back_recv, core_send, core_recv, chip_send,
    chip_recv, z_send, z_recv, quad_send, quad_recv, hi_sem, tab_send, tab_recv, last_sem,
):
    x, y, z, core = place()
    xy = x * 4 + y
    z_hi, member = z // 8, z % 4
    other_core = at(x, y, z, 1 - core)

    def plane(k):
        tx, ty = (x + k // 4) % 4, (y + k % 4) % 4
        return tx * 4 + ty, at(tx, ty, z, core)

    partners = halo_partners()
    partners += [at(x, y, (z + k) % 16, core) for k in (8, 7, 9, 6, 10, 5, 11, 4, 12, 3, 13, 2, 14, 1, 15)]
    partners += [plane(k)[1] for k in FAR_FIRST] + [other_core]
    count = greet(partners)
    owns = [
        pltpu.make_async_copy(cells_part(src, 0, 0), window_part(dst, 0, 0), own_sem.at[i])
        for i, (src, dst) in enumerate(((field_hbm, field_land), (cot_hbm, cot_land)))
    ]
    loads = [
        pltpu.make_async_copy(src, dst, load_sem.at[i])
        for i, (src, dst) in enumerate(
            (
                (table_hbm, table), (sel_hbm, sel), (reg_hbm, reg), (gain_hbm, gain_v),
                (win_hbm, w_in), (feat_hbm, feat), (wout_hbm, w_out),
            )
        )
    ]
    for copy in loads + owns:
        copy.start()
    greeted(count)

    halos = [[], []]
    for i, (src, dst) in enumerate(((field_hbm, field_land), (cot_hbm, cot_land))):
        for quad in (3, 1, 2):
            ha, ho = QUADS[quad]
            halos[i].append(
                remote(
                    cells_part(src, ha, ho), window_part(dst, ha, ho), halo_send.at[i, quad],
                    halo_recv.at[i, quad], window_owner(ha, ho, -1),
                )
            )
    for copy in halos[0]:
        copy.start()
    for copy in loads:
        copy.wait()
    same = same_region(reg, regs) > 0.5
    expand_table(table, sel, tprime, bias)

    owns[0].wait()
    for copy in halos[0]:
        copy.wait_recv()
    for copy in halos[1]:
        copy.start()
    cells_to_rows(field_land, stage)
    cells = stage[...]
    centred = cells - jnp.mean(cells, axis=1, keepdims=True)
    inv_std = lax.rsqrt(jnp.mean(centred * centred, axis=1, keepdims=True) + norm_eps)
    normalized = centred * inv_std
    stage[...] = normalized
    gain = gain_v[...].reshape(1, D)
    normed = (normalized * gain).astype(bf16)
    qkv[:, : 3 * D] = nn(normed, w_in[...]).astype(bf16)
    for i in range(2):
        normt[i] = nt(feat[i], normed).astype(bf16)

    scale = HEAD_DIM ** -0.5
    eye = (iota((128, 128), 0) == iota((128, 128), 1)).astype(bf16)
    lane = iota((CELLS, 128), 1) // HEAD_DIM
    zero = jnp.zeros((CELLS, 128), bf16)

    def part(which, g):
        lo = which * D + g * 128
        return qkv[:, lo : lo + 128]

    def four_heads(a):
        return jnp.concatenate([jnp.where(lane == e, a, zero) for e in range(4)], axis=0)

    for g in range(GROUPS):
        q, k, v = part(0, g), pad_cells(part(1, g)), pad_cells(part(2, g))
        v_t = nt(eye, v).astype(bf16)
        scores = nt(four_heads(q), k)
        for e in range(4):
            h = g * 4 + e
            r = e * HEAD_DIM
            s = scores[e * CELLS : (e + 1) * CELLS] * scale + head_rows(bias, h)
            s = jnp.where(same, s, masked_score)
            s = jnp.exp(s - jnp.max(s, axis=1, keepdims=True))
            p = s * (1.0 / jnp.sum(s, axis=1, keepdims=True))
            probs[h] = p
            att[h * 32 : h * 32 + 32, :] = nt(v_t[r : r + 32], p.astype(bf16)).astype(bf16)
    att_t = [nn(feat[i], att[...]).astype(bf16) for i in range(2)]

    owns[1].wait()
    for copy in halos[1]:
        copy.wait_recv()
    cells_to_rows(cot_land, grad_rows)
    cot = grad_rows[...].astype(bf16)
    qkv[:, 3 * D :] = nt(cot, w_out[...]).astype(bf16)

    def step_refs(g):
        if g < 2:
            return sums.at[g], pair.at[g], mine.at[g], chips.at[g]
        if g == 2:
            return last_sums, last_pair, last_mine, last_chips
        return tsums, tpair, tmine, tchips

    core_copies = []
    for g in range(4):
        src, dst = step_refs(g)[:2]
        core_copies.append(
            remote(src.at[1 - core], dst, core_send.at[g], core_recv.at[g], other_core)
        )
    sends = [[], [], [], []]

    def to_plane(g):
        core_copies[g].wait_recv()
        src, swapped, both, land = step_refs(g)
        both[...] = (src.at[core][...].astype(f32) + swapped[...].astype(f32)).astype(bf16)
        for k in FAR_FIRST:
            index, device = plane(k)
            sends[g].append(
                remote(both.at[index], land.at[k], chip_send.at[g, k], chip_recv.at[g, k], device)
            )
            sends[g][-1].start()

    def from_plane(g):
        _, _, both, land = step_refs(g)
        for copy in sends[g]:
            copy.wait_recv()
        acc = both.at[xy][...].astype(f32)
        for k in range(1, CHIPS):
            acc = acc + land.at[k][...].astype(f32)
        return acc.astype(bf16)

    def pairs(blocks):
        out = []
        for even, odd in zip(blocks[::2], blocks[1::2]):
            even, odd = even.reshape(32, 2, 8, 128), odd.reshape(32, 2, 8, 128)
            out += [even[:, 0], even[:, 1] + odd[:, 0], odd[:, 1]]
        return out

    def put_sums(g, blocks):
        sums[g] = (
            jnp.concatenate(pairs(blocks), axis=1).astype(bf16).reshape(2, CHIPS, 48, 128)
        )
        core_copies[g].start()

    def weight_block(which, g, odd):
        lo = which * D + g * 128
        return nt(normt[odd], dpt[lo : lo + 128, :])

    def grad_scores(g):
        v, do = pad_cells(part(2, g)), part(3, g)
        do_t = nt(eye, do).astype(bf16)
        grad_probs = nt(four_heads(do), v)
        for e in range(4):
            h = g * 4 + e
            r = e * HEAD_DIM
            p = probs[h]
            dp = grad_probs[e * CELLS : (e + 1) * CELLS]
            ds = p * (dp - jnp.sum(p * dp, axis=1, keepdims=True))
            put_head_rows(dsf, h, ds)
            ds_s[h] = (ds * scale).astype(bf16)
            dpt[2 * D + h * 32 : 2 * D + h * 32 + 32, :] = nn(do_t[r : r + 32], p.astype(bf16))[
                :, :CELLS
            ].astype(bf16)

    out_blocks = [nn(att_t[g % 2], cot[:, g * 128 : g * 128 + 128]) for g in range(GROUPS)]
    grad_scores(0)
    put_sums(0, out_blocks + [weight_block(2, 0, 1)])
    grad_scores(1)
    grad_scores(2)

    def grad_heads(g):
        q_t = nt(eye, part(0, g)).astype(bf16)
        k_t = nt(eye, pad_cells(part(1, g))).astype(bf16)
        for e in range(4):
            h = g * 4 + e
            r = e * HEAD_DIM
            ds_low = ds_s[h]
            dpt[h * 32 : h * 32 + 32, :] = nt(k_t[r : r + 32], ds_low).astype(bf16)
            dpt[D + h * 32 : D + h * 32 + 32, :] = nn(q_t[r : r + 32], ds_low)[:, :CELLS].astype(
                bf16
            )

    grad_heads(0)
    put_sums(
        1,
        [weight_block(2, 1, 0), weight_block(2, 2, 1), weight_block(0, 0, 0), weight_block(1, 0, 1)],
    )
    to_plane(0)

    acc = jnp.zeros((192, 2 * HALF_POS), f32)
    for c in range(WIN_LON):
        rows = jnp.concatenate(
            [dsf[pl.ds(half * SCATTER + c * 192, 192), :] for half in range(2)], axis=1
        )
        acc = acc + nt(rows.astype(bf16), sel[c])
    tabf[:, 25 * 128 : 32 * 128] = jnp.zeros((16, 7 * 128), f32)
    for row in range(ROWS):
        for half in range(2):
            off = table_offset(row, half)
            tabf[:, off : off + HALF_POS] = acc[
                row * 16 : row * 16 + 16, half * HALF_POS : (half + 1) * HALF_POS
            ]
    for t in range(32):
        tsums[t // 16, t % 16] = tabf[:, t * 128 : t * 128 + 128].astype(bf16)
    core_copies[3].start()
    to_plane(1)

    grad_heads(1)
    grad_heads(2)

    shifted_t = nn(w_in[...], dpt[...]).astype(bf16)
    eye_c = (iota((CELLS, CELLS), 0) == iota((CELLS, CELLS), 1)).astype(bf16)
    g_normed = nt(eye_c, shifted_t)
    normalized = stage[...]
    grad_gain = jnp.sum(g_normed * normalized, axis=0, keepdims=True)
    extra = jnp.concatenate(
        [grad_gain[:, k * 128 : k * 128 + 128] for k in range(3)] + [jnp.zeros((13, 128), f32)],
        axis=0,
    )
    last_sums[...] = (
        jnp.concatenate(
            pairs([weight_block(i % 2, 1 + i // 2, i % 2) for i in range(4)])
            + [jnp.broadcast_to(extra[None], (32, 16, 128))],
            axis=1,
        )
        .astype(bf16)
        .reshape(2, CHIPS, 64, 128)
    )
    core_copies[2].start()
    to_plane(3)
    scaled = g_normed * gain
    grad_rows[...] = cot.astype(f32) + inv_std * (
        scaled
        - jnp.mean(scaled, axis=1, keepdims=True)
        - normalized * jnp.mean(scaled * normalized, axis=1, keepdims=True)
    )
    to_plane(2)
    for a in range(WIN_LAT):
        for o in range(WIN_LON):
            p = o * ROWS + a * 2
            gwin[a, o] = grad_rows[p : p + 2, :].astype(bf16)
    backs = []
    for quad in (3, 1, 2):
        ha, ho = QUADS[quad]
        backs.append(
            remote(
                window_part(gwin, ha, ho), cells_part(field_out, ha, ho), back_send.at[quad],
                back_recv.at[quad], window_owner(ha, ho, 1),
            )
        )
        backs[-1].start()
    hi_send[...] = from_plane(3)
    hi = remote(hi_send, hi_land, hi_sem.at[0], hi_sem.at[1], at(x, y, (z + 8) % 16, core))
    hi.start()
    for a in range(3):
        for o in range(6):
            field_out[3 + a, 6 + o] = gwin[a, o]

    my_part = (z // 4) * 2 + member % 2

    def keeper(j):
        return (member // 2) * 8 + (z + 4 + j) % 8

    def z_refs(i):
        if i == 0:
            return pack, pack_land, owned, zland
        return last_pack, last_pack_land, last_owned, last_zland

    def to_four(i, select, rows):
        packed, land = z_refs(i)[:2]
        packed[...] = nn(select, rows).astype(bf16).reshape(4, KEEP[i], 128)
        copies = []
        for k in range(1, 4):
            to = (member + k) % 4
            copies.append(
                remote(
                    packed.at[to], land.at[k], quad_send.at[i, k], quad_recv.at[i, k],
                    at(x, y, z - member + to, core),
                )
            )
            copies[-1].start()
        return copies

    def to_keeper(i, j):
        _, _, mine_z, land = z_refs(i)
        return remote(
            mine_z, land.at[my_part], z_send.at[i, j], z_recv.at[i, my_part],
            at(x, y, keeper(j), core),
        )

    def to_keepers(i, copies):
        packed, four, mine_z, land = z_refs(i)
        acc = packed.at[member][...].astype(f32)
        for k in range(1, 4):
            copies[k - 1].wait_recv()
            acc = acc + four[k].astype(f32)
        mine_z[...] = acc.astype(bf16)
        for j in range(8):

            @pl.when(keeper(j) != z)
            def _(j=j):
                to_keeper(i, j).start()

        @pl.when(member // 2 == z_hi)
        def _():
            land[my_part] = mine_z[...]

    def kept(i):
        _, _, mine_z, land = z_refs(i)
        for s in range(8):

            @pl.when((s // 2) * 4 + 2 * z_hi + s % 2 != z)
            def _(s=s):
                remote(mine_z, land.at[s], z_send.at[i, 0], z_recv.at[i, s], other_core).wait_recv()

        lo = i * KEEP[0]
        for half in range(2):
            total = land[half].astype(f32)
            for k in range(1, 4):
                total = total + land[2 * k + half].astype(f32)
            rows_out[half, lo : lo + KEEP[i]] = total

    selects = [keep_rows(8, KEEP[0]), keep_rows(4, KEEP[1])]
    quads = to_four(0, selects[0], jnp.concatenate([from_plane(0), from_plane(1)], axis=0))
    last_quads = to_four(1, selects[1], from_plane(2))
    to_keepers(0, quads)
    to_keepers(1, last_quads)

    hi.wait_recv()
    slot = core * CHIPS + xy
    table_out[slot] = (hi_send[...].astype(f32) + hi_land[...].astype(f32)).astype(bf16)
    tab_copies = []
    for k in FAR_FIRST:
        tab_copies.append(
            remote(
                table_out.at[slot], table_out.at[slot], tab_send.at[k], tab_recv.at[k], plane(k)[1]
            )
        )
        tab_copies[-1].start()

    for copy in tab_copies:
        copy.wait_recv()
    half = table_out.at[pl.ds(core * CHIPS, CHIPS)]
    last = remote(half, half, last_sem.at[0], last_sem.at[1], other_core)
    last.start()
    for copy in backs:
        copy.wait_recv()
    kept(0)
    kept(1)
    last.wait_recv()
    for copy in halos[0] + halos[1] + core_copies + sum(sends, []) + backs + quads + last_quads:
        copy.wait_send()
    for copy in tab_copies + [hi, last]:
        copy.wait_send()
    for i in range(2):
        for j in range(8):

            @pl.when(keeper(j) != z)
            def _(i=i, j=j):
                to_keeper(i, j).wait_send()


def window_call(*args):
    tile = (16, 128)
    grid = (WIN_LAT, WIN_LON, LEV, D)
    sem = pltpu.SemaphoreType.DMA
    return pl.pallas_call(
        window_kernel,
        out_shape=(
            jax.ShapeDtypeStruct(grid, bf16),
            jax.ShapeDtypeStruct((2, KEEP[0] + KEEP[1], 128), f32),
            jax.ShapeDtypeStruct((32,) + tile, bf16),
        ),
        in_specs=[pl.BlockSpec(memory_space=pl.ANY)] * 9,
        out_specs=[pl.BlockSpec(memory_space=VMEM)] * 3,
        scratch_shapes=[
            VMEM(grid, bf16),
            VMEM(grid, bf16),
            VMEM((D,), f32),
            VMEM((D, 3 * D), bf16),
            VMEM((D, D), bf16),
            VMEM((1, HEADS, POS), bf16),
            VMEM((WIN_LAT, LEV, WIN_LON), jnp.int32),
            VMEM((WIN_LON, 2 * HALF_POS, WIDE), bf16),
            VMEM((2, 512, D), bf16),
            VMEM((192, 2 * HALF_POS), f32),
            VMEM((16, 128), f32),
            VMEM((CELLS, D), f32),
            VMEM((CELLS, 4 * D), bf16),
            VMEM((2, 512, CELLS), bf16),
            VMEM((2 * SCATTER, 128), f32),
            VMEM((HEADS, CELLS, WIDE), f32),
            VMEM((2 * SCATTER, 128), f32),
            VMEM((3 * D, CELLS), bf16),
            VMEM((D, CELLS), bf16),
            VMEM((16, 32 * 128), f32),
            VMEM((CELLS, D), f32),
            VMEM(grid, bf16),
            VMEM((2, 2, CHIPS, 48, 128), bf16),
            VMEM((2, CHIPS, 48, 128), bf16),
            VMEM((2, CHIPS, 48, 128), bf16),
            VMEM((2, CHIPS, 48, 128), bf16),
            VMEM((2, CHIPS, 64, 128), bf16),
            VMEM((CHIPS, 64, 128), bf16),
            VMEM((CHIPS, 64, 128), bf16),
            VMEM((CHIPS, 64, 128), bf16),
            VMEM((2, CHIPS) + tile, bf16),
            VMEM((CHIPS,) + tile, bf16),
            VMEM((CHIPS,) + tile, bf16),
            VMEM((CHIPS,) + tile, bf16),
            VMEM((4, KEEP[0], 128), bf16),
            VMEM((4, KEEP[0], 128), bf16),
            VMEM((KEEP[0], 128), bf16),
            VMEM((8, KEEP[0], 128), bf16),
            VMEM((4, KEEP[1], 128), bf16),
            VMEM((4, KEEP[1], 128), bf16),
            VMEM((KEEP[1], 128), bf16),
            VMEM((8, KEEP[1], 128), bf16),
            VMEM(tile, bf16),
            VMEM(tile, bf16),
            VMEM((HEADS, CELLS, WIDE), bf16),
            sem((7,)), sem((2,)), sem((2, 4)), sem((2, 4)), sem((4,)), sem((4,)), sem((4,)),
            sem((4,)), sem((4, CHIPS)), sem((4, CHIPS)), sem((2, 8)), sem((2, 8)),
            sem((2, 4)), sem((2, 4)), sem((2,)), sem((CHIPS,)), sem((CHIPS,)), sem((2,)),
        ],
        compiler_params=pltpu.CompilerParams(
            collective_id=0, has_side_effects=True, vmem_limit_bytes=60 * 1024 * 1024
        ),
        name="window_gradients",
    )(*args)


PIECES = (
    (3, 0), (3, 1), (3, 2), (2, 0), (2, 1), (2, 2), (0, 0), (1, 0), (0, 1), (1, 1), (0, 2), (1, 2),
)


def finish_kernel(field, rows, table, out_field, out_win, out_wout, out_gain, out_table):
    factor = 1.0 / math.sqrt(TOKENS)
    out_field[...] = field[...]
    sums = rows[...] * factor
    for i, (which, g) in enumerate(PIECES):
        half, at_row = (i // 4, (i % 4) * 6) if i < 8 else ((i - 8) // 2, KEEP[0] + (i % 2) * 6)
        part = sums[half, at_row : at_row + 6].astype(bf16)
        if which < 3:
            lo = which * D + g * 128
            out_win[:, lo : lo + 128] = part
        else:
            out_wout[:, g * 128 : g * 128 + 128] = part
    for k in range(3):
        out_gain[k * 128 : k * 128 + 128] = sums[0, KEEP[0] + 12 + k]
    for t in range(TABLE_TILES):
        width = min(128, POS - t * 128)
        values = table[t].astype(f32)
        for h in range(HEADS):
            out_table[h, :, t * 128 : t * 128 + width] = values[h : h + 1, :width]


def finish_call(field, rows, table):
    return pl.pallas_call(
        finish_kernel,
        out_shape=(
            jax.ShapeDtypeStruct((WIN_LAT, WIN_LON, LEV, D), bf16),
            jax.ShapeDtypeStruct((6, 3 * D), bf16),
            jax.ShapeDtypeStruct((6, D), bf16),
            jax.ShapeDtypeStruct((D,), f32),
            jax.ShapeDtypeStruct((HEADS, 1, POS), f32),
        ),
        in_specs=[pl.BlockSpec(memory_space=VMEM)] * 3,
        out_specs=[pl.BlockSpec(memory_space=VMEM)] * 5,
        compiler_params=pltpu.CompilerParams(vmem_limit_bytes=60 * 1024 * 1024),
        name="outputs",
    )(field, rows, table)


def on_device(latent_field, cotangent, norm_gain, input_weight, output_weight, bias_table, regions):
    sel = jnp.asarray(bias_selectors(), bf16)
    feat = jnp.asarray(feature_order(), bf16)
    field, cot = (jnp.transpose(a, (1, 2, 0, 3)) for a in (latent_field, cotangent))
    reg = jnp.transpose(regions, (1, 0, 2))
    sums = window_call(
        field, cot, norm_gain, input_weight, output_weight, bias_table, reg, sel, feat
    )
    grad_field, grad_in, grad_out, grad_gain, table = finish_call(*sums)
    return (
        jnp.transpose(grad_field, (2, 0, 1, 3)),
        grad_in,
        grad_out,
        grad_gain,
        jnp.transpose(table, (1, 0, 2)),
    )


def solution(mesh):
    in_specs = (
        P(None, "lat", "lon", None),
        P(None, "lat", "lon", None),
        P(),
        P(),
        P(),
        P("lat", None, None),
        P(None, "lat", "lon"),
    )
    out_specs = (
        P(None, "lat", "lon", None),
        P("lon", None),
        P("lon", None),
        P(),
        P("lat", None, None),
    )
    return jax.shard_map(
        on_device, mesh=mesh, in_specs=in_specs, out_specs=out_specs, check_vma=False
    )
```

```python
import functools
import math

import jax
import jax.numpy as jnp
import numpy as np
from jax import lax
from jax.experimental import pallas as pl
from jax.experimental.pallas import tpu as pltpu
from jax.sharding import PartitionSpec as P

D = 384
HEADS = 12
HEAD_DIM = 32
LEV = 2
WIN_LAT = 6
WIN_LON = 12
CELLS = 144
ROWS = LEV * WIN_LAT
SPREAD = 2 * WIN_LON - 1
HALF_POS = WIN_LAT * SPREAD
POS = 3312
WIDE = 256
CHIPS = 16
TOKENS = 512 * CELLS
TABLE_TILES = 26
GROUPS = 3
KEEP = (32, 16)
SCATTER = WIN_LON * ROWS * HEADS

norm_eps = 1e-05
masked_score = -1000000000.0
VMEM = pltpu.VMEM
f32 = jnp.float32
bf16 = jnp.bfloat16


def feature_order():
    out = np.zeros((2, 512, D), np.float32)
    for core in range(2):
        for x in range(4):
            for y in range(4):
                for z_hi in range(2):
                    lon = ((x * 2 + z_hi) * 4 + y) * 2 + core
                    for k in range(6):
                        row = ((core * 4 + x) * 4 + y) * 16 + z_hi * 6 + k
                        out[0, row, lon * 6 + k] = 1
                        out[1, row + 4, lon * 6 + k] = 1
    return out


def bias_selectors():
    out = np.zeros((WIN_LON, 2 * HALF_POS, WIDE), np.float32)
    for c in range(WIN_LON):
        for p in range(CELLS):
            d, v, lev = p // ROWS, (p % ROWS) // 2, 1 - p % 2
            out[c, lev * HALF_POS + v * SPREAD + c - d + WIN_LON - 1, p] = 1
    return out


def table_offset(row, y):
    x, u = 1 - row % 2, row // 2
    return ((x * 2 + y) * WIN_LAT + u) * HALF_POS


def head_rows(ref, h):
    return jnp.concatenate(
        [ref[pl.ds(half * SCATTER + h, CELLS, stride=HEADS), :] for half in range(2)], axis=1
    )


def put_head_rows(ref, h, value):
    for half in range(2):
        ref[pl.ds(half * SCATTER + h, CELLS, stride=HEADS), :] = value[:, half * 128 : half * 128 + 128]


def nt(a, b):
    return lax.dot_general(a, b, (((1,), (1,)), ((), ())), preferred_element_type=f32)


def nn(a, b):
    return lax.dot_general(a, b, (((1,), (0,)), ((), ())), preferred_element_type=f32)


def tn(a, b):
    return lax.dot_general(a, b, (((0,), (0,)), ((), ())), preferred_element_type=f32)


def iota(shape, dim):
    return lax.broadcasted_iota(jnp.int32, shape, dim)


def place():
    lon, lat = lax.axis_index("lon"), lax.axis_index("lat")
    x, z_hi, y, core = lon // 16, (lon // 8) % 2, (lon // 2) % 4, lon % 2
    return x, y, z_hi * 8 + lat, core


def at(x, y, z, core):
    return {"lon": ((x * 2 + z // 8) * 4 + y) * 2 + core, "lat": z % 8}


def window_owner(ha, ho, sign):
    lon, lat = lax.axis_index("lon"), lax.axis_index("lat")
    return {"lon": (lon + sign * ho + 64) % 64, "lat": (lat + sign * ha + 8) % 8}


def greet(partners):
    barrier = pltpu.get_barrier_semaphore()
    for partner in partners:
        pl.semaphore_signal(barrier, inc=1, device_id=partner, device_id_type=pl.DeviceIdType.MESH)
    return len(partners)


def greeted(count):
    pl.semaphore_wait(pltpu.get_barrier_semaphore(), count)


def remote(src, dst, send, recv, device):
    return pltpu.make_async_remote_copy(
        src_ref=src, dst_ref=dst, send_sem=send, recv_sem=recv, device_id=device,
        device_id_type=pl.DeviceIdType.MESH,
    )


QUADS = ((0, 0), (0, 1), (1, 0), (1, 1))


def cells_part(ref, ha, ho):
    return ref.at[pl.ds(3 * (1 - ha), 3), pl.ds(6 * (1 - ho), 6)]


def window_part(ref, ha, ho):
    return ref.at[pl.ds(3 * ha, 3), pl.ds(6 * ho, 6)]


def halo_partners():
    return [window_owner(ha, ho, sign) for ha, ho in QUADS[1:] for sign in (-1, 1)]


def expand_table(table, sel_ref, tprime, bias):
    table = table[0].astype(f32)
    tprime[...] = jnp.zeros_like(tprime)
    for row in range(ROWS):
        for y in range(2):
            off = table_offset(row, y)
            tprime[row * HEADS : (row + 1) * HEADS, y * HALF_POS : (y + 1) * HALF_POS] = table[
                :, off : off + HALF_POS
            ]
    rows = tprime[...].astype(bf16)
    for c in range(WIN_LON):
        part = nn(rows, sel_ref[c])
        for half in range(2):
            base = half * SCATTER + c * CELLS
            bias[base : base + CELLS, :] = part[:, half * 128 : half * 128 + 128]


def same_region(reg, regs):
    for a in range(WIN_LAT):
        for lev in range(2):
            regs[a * 2 + lev : a * 2 + lev + 1, 0:WIN_LON] = reg[a, 1 - lev : 2 - lev].astype(f32)
    grid = regs[0:ROWS, 0:WIN_LON].astype(bf16)
    where = iota((ROWS, WIDE), 1)
    spread = nn(grid, (where // ROWS == iota((ROWS, WIDE), 0)).astype(bf16))
    row = jnp.sum(
        jnp.where(where % ROWS == iota((ROWS, WIDE), 0), spread, 0.0), axis=0, keepdims=True
    )
    kind = iota((16, WIDE), 0).astype(f32)
    hot = jnp.where((row == kind) & (iota((16, WIDE), 1) < CELLS), 1.0, 0.0)
    return tn(hot[:, :CELLS].astype(bf16), hot.astype(bf16))


def cells_to_rows(land, stage):
    for a in range(WIN_LAT):
        for o in range(WIN_LON):
            p = o * ROWS + a * 2
            stage[p : p + 2, :] = land[a, o].astype(f32)


def pad_cells(a):
    return jnp.concatenate([a, jnp.zeros((WIDE - CELLS, a.shape[1]), a.dtype)], axis=0)


def keep_rows(pieces, rows):
    shape = (4 * rows, pieces * 12 + (16 if pieces == 4 else 0))
    row, col = iota(shape, 0), iota(shape, 1)
    part, w = row // rows, row % rows
    mine = pieces // 2 * 6
    own = ((part % 2) * (pieces // 2) + w // 6) * 12 + (part // 2) * 6 + w % 6
    gain = jnp.where((part % 2 == 0) & (w < mine + 3), pieces * 12 + w - mine, -1)
    return (col == jnp.where(w < mine, own, gain if pieces == 4 else -1)).astype(bf16)


FAR_FIRST = (10, 6, 9, 11, 14, 2, 8, 5, 7, 13, 15, 1, 3, 4, 12)


def window_kernel(
    field_hbm, cot_hbm, gain_hbm, win_hbm, wout_hbm, table_hbm, reg_hbm, sel_hbm, feat_hbm,
    field_out, rows_out, table_out,
    field_land, cot_land, gain_v, w_in, w_out, table, reg, sel, feat, tprime, regs, stage,
    qkv, normt, bias, probs, dsf, dpt, att, tabf, grad_rows, gwin,
    sums, pair, mine, chips, last_sums, last_pair, last_mine, last_chips, tsums, tpair, tmine, tchips,
    pack, pack_land, owned, zland, last_pack, last_pack_land, last_owned, last_zland, hi_send, hi_land,
    ds_s,
    load_sem, own_sem, halo_send, halo_recv, back_send, back_recv, core_send, core_recv, chip_send,
    chip_recv, z_send, z_recv, quad_send, quad_recv, hi_sem, tab_send, tab_recv, last_sem,
):
    x, y, z, core = place()
    xy = x * 4 + y
    z_hi, member = z // 8, z % 4
    other_core = at(x, y, z, 1 - core)

    def plane(k):
        tx, ty = (x + k // 4) % 4, (y + k % 4) % 4
        return tx * 4 + ty, at(tx, ty, z, core)

    partners = halo_partners()
    partners += [at(x, y, (z + k) % 16, core) for k in (8, 7, 9, 6, 10, 5, 11, 4, 12, 3, 13, 2, 14, 1, 15)]
    partners += [plane(k)[1] for k in FAR_FIRST] + [other_core]
    count = greet(partners)
    owns = [
        pltpu.make_async_copy(cells_part(src, 0, 0), window_part(dst, 0, 0), own_sem.at[i])
        for i, (src, dst) in enumerate(((field_hbm, field_land), (cot_hbm, cot_land)))
    ]
    loads = [
        pltpu.make_async_copy(src, dst, load_sem.at[i])
        for i, (src, dst) in enumerate(
            (
                (table_hbm, table), (sel_hbm, sel), (reg_hbm, reg), (gain_hbm, gain_v),
                (win_hbm, w_in), (feat_hbm, feat), (wout_hbm, w_out),
            )
        )
    ]
    for copy in loads + owns:
        copy.start()
    greeted(count)

    halos = [[], []]
    for i, (src, dst) in enumerate(((field_hbm, field_land), (cot_hbm, cot_land))):
        for quad in (3, 1, 2):
            ha, ho = QUADS[quad]
            halos[i].append(
                remote(
                    cells_part(src, ha, ho), window_part(dst, ha, ho), halo_send.at[i, quad],
                    halo_recv.at[i, quad], window_owner(ha, ho, -1),
                )
            )
    for copy in halos[0]:
        copy.start()
    for copy in loads:
        copy.wait()
    same = same_region(reg, regs) > 0.5
    expand_table(table, sel, tprime, bias)

    owns[0].wait()
    for copy in halos[0]:
        copy.wait_recv()
    for copy in halos[1]:
        copy.start()
    cells_to_rows(field_land, stage)
    cells = stage[...]
    centred = cells - jnp.mean(cells, axis=1, keepdims=True)
    inv_std = lax.rsqrt(jnp.mean(centred * centred, axis=1, keepdims=True) + norm_eps)
    normalized = centred * inv_std
    stage[...] = normalized
    gain = gain_v[...].reshape(1, D)
    normed = (normalized * gain).astype(bf16)
    qkv[:, : 3 * D] = nn(normed, w_in[...]).astype(bf16)
    for i in range(2):
        normt[i] = nt(feat[i], normed).astype(bf16)

    scale = HEAD_DIM ** -0.5
    eye = (iota((128, 128), 0) == iota((128, 128), 1)).astype(bf16)
    lane = iota((CELLS, 128), 1) // HEAD_DIM
    zero = jnp.zeros((CELLS, 128), bf16)

    def part(which, g):
        lo = which * D + g * 128
        return qkv[:, lo : lo + 128]

    def four_heads(a):
        return jnp.concatenate([jnp.where(lane == e, a, zero) for e in range(4)], axis=0)

    for g in range(GROUPS):
        q, k, v = part(0, g), pad_cells(part(1, g)), pad_cells(part(2, g))
        v_t = nt(eye, v).astype(bf16)
        scores = nt(four_heads(q), k)
        for e in range(4):
            h = g * 4 + e
            r = e * HEAD_DIM
            s = scores[e * CELLS : (e + 1) * CELLS] * scale + head_rows(bias, h)
            s = jnp.where(same, s, masked_score)
            s = jnp.exp(s - jnp.max(s, axis=1, keepdims=True))
            p = s * (1.0 / jnp.sum(s, axis=1, keepdims=True))
            probs[h] = p
            att[h * 32 : h * 32 + 32, :] = nt(v_t[r : r + 32], p.astype(bf16)).astype(bf16)
    att_t = [nn(feat[i], att[...]).astype(bf16) for i in range(2)]

    owns[1].wait()
    for copy in halos[1]:
        copy.wait_recv()
    cells_to_rows(cot_land, grad_rows)
    cot = grad_rows[...].astype(bf16)
    qkv[:, 3 * D :] = nt(cot, w_out[...]).astype(bf16)

    def step_refs(g):
        if g < 2:
            return sums.at[g], pair.at[g], mine.at[g], chips.at[g]
        if g == 2:
            return last_sums, last_pair, last_mine, last_chips
        return tsums, tpair, tmine, tchips

    core_copies = []
    for g in range(4):
        src, dst = step_refs(g)[:2]
        core_copies.append(
            remote(src.at[1 - core], dst, core_send.at[g], core_recv.at[g], other_core)
        )
    sends = [[], [], [], []]

    def to_plane(g):
        core_copies[g].wait_recv()
        src, swapped, both, land = step_refs(g)
        both[...] = (src.at[core][...].astype(f32) + swapped[...].astype(f32)).astype(bf16)
        for k in FAR_FIRST:
            index, device = plane(k)
            sends[g].append(
                remote(both.at[index], land.at[k], chip_send.at[g, k], chip_recv.at[g, k], device)
            )
            sends[g][-1].start()

    def from_plane(g):
        _, _, both, land = step_refs(g)
        for copy in sends[g]:
            copy.wait_recv()
        acc = both.at[xy][...].astype(f32)
        for k in range(1, CHIPS):
            acc = acc + land.at[k][...].astype(f32)
        return acc.astype(bf16)

    def pairs(blocks):
        out = []
        for even, odd in zip(blocks[::2], blocks[1::2]):
            even, odd = even.reshape(32, 2, 8, 128), odd.reshape(32, 2, 8, 128)
            out += [even[:, 0], even[:, 1] + odd[:, 0], odd[:, 1]]
        return out

    def put_sums(g, blocks):
        sums[g] = (
            jnp.concatenate(pairs(blocks), axis=1).astype(bf16).reshape(2, CHIPS, 48, 128)
        )
        core_copies[g].start()

    def weight_block(which, g, odd):
        lo = which * D + g * 128
        return nt(normt[odd], dpt[lo : lo + 128, :])

    def grad_scores(g):
        v, do = pad_cells(part(2, g)), part(3, g)
        do_t = nt(eye, do).astype(bf16)
        grad_probs = nt(four_heads(do), v)
        for e in range(4):
            h = g * 4 + e
            r = e * HEAD_DIM
            p = probs[h]
            dp = grad_probs[e * CELLS : (e + 1) * CELLS]
            ds = p * (dp - jnp.sum(p * dp, axis=1, keepdims=True))
            put_head_rows(dsf, h, ds)
            ds_s[h] = (ds * scale).astype(bf16)
            dpt[2 * D + h * 32 : 2 * D + h * 32 + 32, :] = nn(do_t[r : r + 32], p.astype(bf16))[
                :, :CELLS
            ].astype(bf16)

    out_blocks = [nn(att_t[g % 2], cot[:, g * 128 : g * 128 + 128]) for g in range(GROUPS)]
    grad_scores(0)
    put_sums(0, out_blocks + [weight_block(2, 0, 1)])
    grad_scores(1)
    grad_scores(2)

    def grad_heads(g):
        q_t = nt(eye, part(0, g)).astype(bf16)
        k_t = nt(eye, pad_cells(part(1, g))).astype(bf16)
        for e in range(4):
            h = g * 4 + e
            r = e * HEAD_DIM
            ds_low = ds_s[h]
            dpt[h * 32 : h * 32 + 32, :] = nt(k_t[r : r + 32], ds_low).astype(bf16)
            dpt[D + h * 32 : D + h * 32 + 32, :] = nn(q_t[r : r + 32], ds_low)[:, :CELLS].astype(
                bf16
            )

    grad_heads(0)
    put_sums(
        1,
        [weight_block(2, 1, 0), weight_block(2, 2, 1), weight_block(0, 0, 0), weight_block(1, 0, 1)],
    )
    to_plane(0)

    acc = jnp.zeros((CELLS, 2 * HALF_POS), f32)
    for c in range(WIN_LON):
        rows = jnp.concatenate(
            [dsf[pl.ds(half * SCATTER + c * CELLS, CELLS), :] for half in range(2)], axis=1
        )
        acc = acc + nt(rows.astype(bf16), sel[c])
    tabf[...] = jnp.zeros_like(tabf)
    for row in range(ROWS):
        for half in range(2):
            off = table_offset(row, half)
            tabf[0:HEADS, off : off + HALF_POS] = acc[
                row * HEADS : (row + 1) * HEADS, half * HALF_POS : (half + 1) * HALF_POS
            ]
    for t in range(32):
        tsums[t // 16, t % 16] = tabf[:, t * 128 : t * 128 + 128].astype(bf16)
    core_copies[3].start()
    to_plane(1)

    grad_heads(1)
    grad_heads(2)

    shifted_t = nn(w_in[...], dpt[...]).astype(bf16)
    eye_c = (iota((CELLS, CELLS), 0) == iota((CELLS, CELLS), 1)).astype(bf16)
    g_normed = nt(eye_c, shifted_t)
    normalized = stage[...]
    grad_gain = jnp.sum(g_normed * normalized, axis=0, keepdims=True)
    extra = jnp.concatenate(
        [grad_gain[:, k * 128 : k * 128 + 128] for k in range(3)] + [jnp.zeros((13, 128), f32)],
        axis=0,
    )
    last_sums[...] = (
        jnp.concatenate(
            pairs([weight_block(i % 2, 1 + i // 2, i % 2) for i in range(4)])
            + [jnp.broadcast_to(extra[None], (32, 16, 128))],
            axis=1,
        )
        .astype(bf16)
        .reshape(2, CHIPS, 64, 128)
    )
    core_copies[2].start()
    to_plane(3)
    scaled = g_normed * gain
    grad_rows[...] = cot.astype(f32) + inv_std * (
        scaled
        - jnp.mean(scaled, axis=1, keepdims=True)
        - normalized * jnp.mean(scaled * normalized, axis=1, keepdims=True)
    )
    to_plane(2)
    for a in range(WIN_LAT):
        for o in range(WIN_LON):
            p = o * ROWS + a * 2
            gwin[a, o] = grad_rows[p : p + 2, :].astype(bf16)
    backs = []
    for quad in (3, 1, 2):
        ha, ho = QUADS[quad]
        backs.append(
            remote(
                window_part(gwin, ha, ho), cells_part(field_out, ha, ho), back_send.at[quad],
                back_recv.at[quad], window_owner(ha, ho, 1),
            )
        )
        backs[-1].start()
    hi_send[...] = from_plane(3)
    hi = remote(hi_send, hi_land, hi_sem.at[0], hi_sem.at[1], at(x, y, (z + 8) % 16, core))
    hi.start()
    for a in range(3):
        for o in range(6):
            field_out[3 + a, 6 + o] = gwin[a, o]

    my_part = (z // 4) * 2 + member % 2

    def keeper(j):
        return (member // 2) * 8 + (z + 4 + j) % 8

    def z_refs(i):
        if i == 0:
            return pack, pack_land, owned, zland
        return last_pack, last_pack_land, last_owned, last_zland

    def to_four(i, select, rows):
        packed, land = z_refs(i)[:2]
        packed[...] = nn(select, rows).astype(bf16).reshape(4, KEEP[i], 128)
        copies = []
        for k in range(1, 4):
            to = (member + k) % 4
            copies.append(
                remote(
                    packed.at[to], land.at[k], quad_send.at[i, k], quad_recv.at[i, k],
                    at(x, y, z - member + to, core),
                )
            )
            copies[-1].start()
        return copies

    def to_keeper(i, j):
        _, _, mine_z, land = z_refs(i)
        return remote(
            mine_z, land.at[my_part], z_send.at[i, j], z_recv.at[i, my_part],
            at(x, y, keeper(j), core),
        )

    def to_keepers(i, copies):
        packed, four, mine_z, land = z_refs(i)
        acc = packed.at[member][...].astype(f32)
        for k in range(1, 4):
            copies[k - 1].wait_recv()
            acc = acc + four[k].astype(f32)
        mine_z[...] = acc.astype(bf16)
        for j in range(8):

            @pl.when(keeper(j) != z)
            def _(j=j):
                to_keeper(i, j).start()

        @pl.when(member // 2 == z_hi)
        def _():
            land[my_part] = mine_z[...]

    def kept(i):
        _, _, mine_z, land = z_refs(i)
        for s in range(8):

            @pl.when((s // 2) * 4 + 2 * z_hi + s % 2 != z)
            def _(s=s):
                remote(mine_z, land.at[s], z_send.at[i, 0], z_recv.at[i, s], other_core).wait_recv()

        lo = i * KEEP[0]
        for half in range(2):
            total = land[half].astype(f32)
            for k in range(1, 4):
                total = total + land[2 * k + half].astype(f32)
            rows_out[half, lo : lo + KEEP[i]] = total

    selects = [keep_rows(8, KEEP[0]), keep_rows(4, KEEP[1])]
    quads = to_four(0, selects[0], jnp.concatenate([from_plane(0), from_plane(1)], axis=0))
    last_quads = to_four(1, selects[1], from_plane(2))
    to_keepers(0, quads)
    to_keepers(1, last_quads)

    hi.wait_recv()
    slot = core * CHIPS + xy
    table_out[slot] = (hi_send[...].astype(f32) + hi_land[...].astype(f32)).astype(bf16)
    tab_copies = []
    for k in FAR_FIRST:
        tab_copies.append(
            remote(
                table_out.at[slot], table_out.at[slot], tab_send.at[k], tab_recv.at[k], plane(k)[1]
            )
        )
        tab_copies[-1].start()

    for copy in tab_copies:
        copy.wait_recv()
    half = table_out.at[pl.ds(core * CHIPS, CHIPS)]
    last = remote(half, half, last_sem.at[0], last_sem.at[1], other_core)
    last.start()
    for copy in backs:
        copy.wait_recv()
    kept(0)
    kept(1)
    last.wait_recv()
    for copy in halos[0] + halos[1] + core_copies + sum(sends, []) + backs + quads + last_quads:
        copy.wait_send()
    for copy in tab_copies + [hi, last]:
        copy.wait_send()
    for i in range(2):
        for j in range(8):

            @pl.when(keeper(j) != z)
            def _(i=i, j=j):
                to_keeper(i, j).wait_send()


def window_call(*args):
    tile = (16, 128)
    grid = (WIN_LAT, WIN_LON, LEV, D)
    sem = pltpu.SemaphoreType.DMA
    return pl.pallas_call(
        window_kernel,
        out_shape=(
            jax.ShapeDtypeStruct(grid, bf16),
            jax.ShapeDtypeStruct((2, KEEP[0] + KEEP[1], 128), f32),
            jax.ShapeDtypeStruct((32,) + tile, bf16),
        ),
        in_specs=[pl.BlockSpec(memory_space=pl.ANY)] * 9,
        out_specs=[pl.BlockSpec(memory_space=VMEM)] * 3,
        scratch_shapes=[
            VMEM(grid, bf16),
            VMEM(grid, bf16),
            VMEM((D,), f32),
            VMEM((D, 3 * D), bf16),
            VMEM((D, D), bf16),
            VMEM((1, HEADS, POS), bf16),
            VMEM((WIN_LAT, LEV, WIN_LON), jnp.int32),
            VMEM((WIN_LON, 2 * HALF_POS, WIDE), bf16),
            VMEM((2, 512, D), bf16),
            VMEM((CELLS, 2 * HALF_POS), f32),
            VMEM((16, 128), f32),
            VMEM((CELLS, D), f32),
            VMEM((CELLS, 4 * D), bf16),
            VMEM((2, 512, CELLS), bf16),
            VMEM((2 * SCATTER, 128), f32),
            VMEM((HEADS, CELLS, WIDE), f32),
            VMEM((2 * SCATTER, 128), f32),
            VMEM((3 * D, CELLS), bf16),
            VMEM((D, CELLS), bf16),
            VMEM((16, 32 * 128), f32),
            VMEM((CELLS, D), f32),
            VMEM(grid, bf16),
            VMEM((2, 2, CHIPS, 48, 128), bf16),
            VMEM((2, CHIPS, 48, 128), bf16),
            VMEM((2, CHIPS, 48, 128), bf16),
            VMEM((2, CHIPS, 48, 128), bf16),
            VMEM((2, CHIPS, 64, 128), bf16),
            VMEM((CHIPS, 64, 128), bf16),
            VMEM((CHIPS, 64, 128), bf16),
            VMEM((CHIPS, 64, 128), bf16),
            VMEM((2, CHIPS) + tile, bf16),
            VMEM((CHIPS,) + tile, bf16),
            VMEM((CHIPS,) + tile, bf16),
            VMEM((CHIPS,) + tile, bf16),
            VMEM((4, KEEP[0], 128), bf16),
            VMEM((4, KEEP[0], 128), bf16),
            VMEM((KEEP[0], 128), bf16),
            VMEM((8, KEEP[0], 128), bf16),
            VMEM((4, KEEP[1], 128), bf16),
            VMEM((4, KEEP[1], 128), bf16),
            VMEM((KEEP[1], 128), bf16),
            VMEM((8, KEEP[1], 128), bf16),
            VMEM(tile, bf16),
            VMEM(tile, bf16),
            VMEM((HEADS, CELLS, WIDE), bf16),
            sem((7,)), sem((2,)), sem((2, 4)), sem((2, 4)), sem((4,)), sem((4,)), sem((4,)),
            sem((4,)), sem((4, CHIPS)), sem((4, CHIPS)), sem((2, 8)), sem((2, 8)),
            sem((2, 4)), sem((2, 4)), sem((2,)), sem((CHIPS,)), sem((CHIPS,)), sem((2,)),
        ],
        compiler_params=pltpu.CompilerParams(
            collective_id=0, has_side_effects=True, vmem_limit_bytes=60 * 1024 * 1024
        ),
        name="window_gradients",
    )(*args)


PIECES = (
    (3, 0), (3, 1), (3, 2), (2, 0), (2, 1), (2, 2), (0, 0), (1, 0), (0, 1), (1, 1), (0, 2), (1, 2),
)


def finish_kernel(field, rows, table, out_field, out_win, out_wout, out_gain, out_table):
    factor = 1.0 / math.sqrt(TOKENS)
    out_field[...] = field[...]
    sums = rows[...] * factor
    for i, (which, g) in enumerate(PIECES):
        half, at_row = (i // 4, (i % 4) * 6) if i < 8 else ((i - 8) // 2, KEEP[0] + (i % 2) * 6)
        part = sums[half, at_row : at_row + 6].astype(bf16)
        if which < 3:
            lo = which * D + g * 128
            out_win[:, lo : lo + 128] = part
        else:
            out_wout[:, g * 128 : g * 128 + 128] = part
    for k in range(3):
        out_gain[k * 128 : k * 128 + 128] = sums[0, KEEP[0] + 12 + k]
    for t in range(TABLE_TILES):
        width = min(128, POS - t * 128)
        values = table[t].astype(f32)
        for h in range(HEADS):
            out_table[h, :, t * 128 : t * 128 + width] = values[h : h + 1, :width]


def finish_call(field, rows, table):
    return pl.pallas_call(
        finish_kernel,
        out_shape=(
            jax.ShapeDtypeStruct((WIN_LAT, WIN_LON, LEV, D), bf16),
            jax.ShapeDtypeStruct((6, 3 * D), bf16),
            jax.ShapeDtypeStruct((6, D), bf16),
            jax.ShapeDtypeStruct((D,), f32),
            jax.ShapeDtypeStruct((HEADS, 1, POS), f32),
        ),
        in_specs=[pl.BlockSpec(memory_space=VMEM)] * 3,
        out_specs=[pl.BlockSpec(memory_space=VMEM)] * 5,
        compiler_params=pltpu.CompilerParams(vmem_limit_bytes=60 * 1024 * 1024),
        name="outputs",
    )(field, rows, table)


def on_device(latent_field, cotangent, norm_gain, input_weight, output_weight, bias_table, regions):
    sel = jnp.asarray(bias_selectors(), bf16)
    feat = jnp.asarray(feature_order(), bf16)
    field, cot = (jnp.transpose(a, (1, 2, 0, 3)) for a in (latent_field, cotangent))
    reg = jnp.transpose(regions, (1, 0, 2))
    sums = window_call(
        field, cot, norm_gain, input_weight, output_weight, bias_table, reg, sel, feat
    )
    grad_field, grad_in, grad_out, grad_gain, table = finish_call(*sums)
    return (
        jnp.transpose(grad_field, (2, 0, 1, 3)),
        grad_in,
        grad_out,
        grad_gain,
        jnp.transpose(table, (1, 0, 2)),
    )


def solution(mesh):
    in_specs = (
        P(None, "lat", "lon", None),
        P(None, "lat", "lon", None),
        P(),
        P(),
        P(),
        P("lat", None, None),
        P(None, "lat", "lon"),
    )
    out_specs = (
        P(None, "lat", "lon", None),
        P("lon", None),
        P("lon", None),
        P(),
        P("lat", None, None),
    )
    return jax.shard_map(
        on_device, mesh=mesh, in_specs=in_specs, out_specs=out_specs, check_vma=False
    )
```
